1024 devices in a mesh: node: 32 (over x, z_hi, core), feat: 32 (over z_lo, y).
Axes of the slice: x: 4, y: 4, z: 32 (z_hi: 4, z_lo: 8; z = z_hi * 8 + z_lo), core: 2. Of those that a mesh axis runs over, the one named last changes fastest.
Arguments:
- features: bfloat16 [768, 131072], P('feat', 'node'), may hold values from -6 to 6
- counts: int32 [512], P('node'), may hold values from 1 to 3
- src_owner: int32 [1536, 1], P('node'), may hold values from 0 to 31; in each aligned block of 48 rows (0 to 47, 48 to 95, ...) at most 4 rows name the same one
- src_local: int32 [1536], P('node'), may hold values from 0 to 15
- tiles: bfloat16 [1536, 256, 256], P('node'), may hold values from -0.375 to 0.375
- w_neigh: bfloat16 [768, 512], replicated, may hold values from -0.21875 to 0.21875
- self_part: bfloat16 [512, 131072], P(None, ('node', 'feat')), may hold values from -6 to 6
- cotangent: bfloat16 [512, 131072], P(None, ('node', 'feat')), may hold values from -24 to 24
Outputs:
- hidden: bfloat16 [512, 131072], P(None, ('node', 'feat'))
- grad_neigh: float32 [512, 768], P('feat', 'node')
The draws below stay inside these ranges and needn't reach their ends.
Inputs may be any that keep to these rules, and one draw needn't show every extreme that they name: `src_owner`: within the 48 slots of one node device (aligned blocks of rows), no owner is named by more than 4 slots.
All inputs are finite; a program needn't handle non-finite values.
Results may differ from the reference program's by a relative error of at most 0.0052.
Values may be sent and summed in bfloat16 or wider, within the bound.
No kernel may reach another device: no remote copies, remote signals or barrier semaphores. Data moves between devices by JAX's collectives and lax.ppermute only.
A program may use at most 64 MiB of HBM per device.

```python
import math
import jax
import jax.numpy as jnp
import numpy as np
from jax import lax

F = 768
HID = 512
TB = 256
MAXT = 3
NB_DEV = 16
NBLK = 512
NODES = 131072
CAP = 4
N_NODE = 32


def with_ends(result, own_key, least, high):
    spot = [jax.random.randint(jax.random.fold_in(own_key, axis), (), 0, length) for axis, length in enumerate(result.shape)]
    main_axis = result.shape.index(max(result.shape))
    next_to = spot[:main_axis] + [(spot[main_axis] + 1) % result.shape[main_axis]] + spot[main_axis + 1:]
    return result.at[tuple(spot)].set(least).at[tuple(next_to)].set(high)


def spiked(drawn, rng, source, target, shards_of, factor):
    owner, partner = [(jnp.arange(drawn.shape[axis_at]) // (drawn.shape[axis_at] // shards_of)).reshape([-1 if axis == axis_at else 1 for axis in range(drawn.ndim)]) for axis_at in (source, target)]
    chosen = jax.random.permutation(rng, shards_of)[partner]
    strong = (owner == chosen) | (owner == (partner + shards_of // 2) % shards_of)
    return jnp.where(strong, factor * drawn, drawn)


def block_scale(key, shape, cuts, least, high):
    factor_of = 1.0
    for position, blocks in cuts:
        steps = jax.random.uniform(jax.random.fold_in(jax.random.fold_in(key, 6), position), (blocks,), jnp.float32, least / len(cuts), high / len(cuts))
        factor_of = factor_of * jnp.repeat(jnp.exp(steps), shape[position] // blocks).reshape((-1,) + (1,) * (len(shape) - 1 - position))
    return factor_of


def deal_out(own_key, own, number, rows, count, top, limit, slope):
    ranking = jax.random.permutation(own_key, count)
    crowded, common = portions_of(count, rows * top, limit, slope, True), portions_of(count, rows * top, limit, slope, False)
    places = jnp.arange(count)

    def named(tallies, offset_by):
        used = int((tallies > 0).sum())
        fixed = max(1, used // 4)
        shifted = fixed + (places - fixed + offset_by * (used - fixed)) % max(1, count - fixed)
        return jnp.zeros((count,), jnp.int32).at[ranking[jnp.where(places < fixed, places, shifted)]].set(jnp.asarray(tallies, jnp.int32))

    tallies = jnp.where(number % 4 == 0, named(crowded, number // 4), named(common, number - number // 4 - 1))
    mixed = jax.random.permutation(jax.random.fold_in(own, 3), count)
    donor, taker = mixed[0:count // 2 * 2:2], mixed[1:count // 2 * 2:2]
    margin = jnp.minimum(tallies[donor] - 1, limit - tallies[taker]) // 2
    margin = jnp.where((donor == ranking[0]) | (taker == ranking[0]) | (tallies[taker] == 0), 0, jnp.maximum(margin, 0))
    shifted = jax.random.randint(jax.random.fold_in(own, 4), (count // 2,), 0, 1 << 20) % (margin + 1)
    tallies = tallies.at[donor].add(-shifted).at[taker].add(shifted)
    members = jnp.searchsorted(jnp.cumsum(tallies), jnp.arange(rows * top), side="right").astype(jnp.int32)
    listing = members.reshape(top, rows).T
    listing = listing[jax.random.permutation(jax.random.fold_in(own, 1), rows)]
    offset_by = jax.random.randint(jax.random.fold_in(own, 2), (rows, 1), 0, top)
    return jnp.take_along_axis(listing, (jnp.arange(top)[None, :] + offset_by) % top, axis=1)


def portions_of(count, total, most, skew, full):
    portions = [(1 << 20) // math.isqrt(grade ** skew) + 1 for grade in range(1, count + 1)]
    largest = most if full else min(most, max(-(-total // count), total * portions[0] // sum(portions)))
    least = 1 if total - largest >= count - 1 else 0
    given, spare = [largest] + [least] * (count - 1), total - largest - least * (count - 1)
    while spare > 0:
        candidates = [i for i in range(1, count) if given[i] < largest] or [i for i in range(1, count) if given[i] < most]
        pool, remaining = sum([portions[i] for i in candidates]), spare
        for i in candidates:
            more = min(most - given[i], max(1, remaining * portions[i] // pool), spare)
            given[i] = given[i] + more
            spare = spare - more
    return np.array(given)


def normal_values(rng, shape, spread, limit, split=(), kind=jnp.bfloat16):
    gain = block_scale(rng, shape, split, -0.22, 0.18) if split else 1.0
    drawn = jax.random.normal(rng, shape, jnp.float32) * spread * gain
    return jnp.minimum(jnp.maximum(drawn, -limit), limit).astype(kind)


def noise_with(stream_key, shape, deviation, most, cuts, heavy, kind=jnp.bfloat16):
    drawn = deviation * jax.random.normal(stream_key, shape, jnp.float32)
    if cuts:
        drawn = drawn * block_scale(stream_key, shape, cuts, -0.22, 0.18)
    return jnp.clip(spiked(drawn, jax.random.fold_in(stream_key, 3), *heavy), -most, most).astype(kind)


def setup_inputs(seed: int = 0) -> dict:
    streams_of = jax.random.split(jax.random.key(seed), 9)
    features = normal_values(streams_of[0], (F, NODES), 1.0, 6.0, ((0, 32), (1, 32)))
    counts = with_ends(jax.random.randint(streams_of[1], (NBLK,), 1, MAXT + 1), jax.random.fold_in(streams_of[1], 1), 1, MAXT).astype(jnp.int32)
    src_owner_keys = jax.random.split(jax.random.fold_in(streams_of[2], 1), (NBLK * MAXT) // (NB_DEV * MAXT))
    src_owner_turns = jax.random.permutation(jax.random.fold_in(streams_of[2], 3), (NBLK * MAXT) // (NB_DEV * MAXT))
    src_owner = jax.vmap(lambda own, number: deal_out(jax.random.fold_in(streams_of[2], 2), own, number, NB_DEV * MAXT, N_NODE, 1, CAP, 2))(src_owner_keys, src_owner_turns).reshape((NBLK * MAXT, 1))
    src_local = with_ends(jax.random.randint(streams_of[3], (NBLK * MAXT,), 0, NB_DEV), jax.random.fold_in(streams_of[3], 1), 0, NB_DEV - 1).astype(jnp.int32)
    tiles = normal_values(streams_of[4], (NBLK * MAXT, TB, TB), TB ** -0.5, 0.375, ((0, 32),))
    w_neigh = normal_values(streams_of[5], (F, HID), F ** -0.5, 0.21875)
    self_part = normal_values(streams_of[6], (HID, NODES), 1.0, 6.0, ((1, 1024),))
    cotangent = noise_with(streams_of[7], (HID, NODES), 1.0, 24.0, ((1, 1024),), (1, 0, 512, 6.0))
    return {"features": features, "counts": counts, "src_owner": src_owner, "src_local": src_local, "tiles": tiles, "w_neigh": w_neigh, "self_part": self_part, "cotangent": cotangent}


def silu_slope(values):
    sig = jax.nn.sigmoid(values)
    return sig * (1.0 + values * (1.0 - sig))

def reference(features, counts, src_owner, src_local, tiles, w_neigh, self_part, cotangent):
    blocks = features.reshape(F, NBLK, TB)

    def one_device(inputs):
        dev_counts, dev_owner, dev_local, dev_tiles = inputs
        source_pos = (dev_owner * NB_DEV + dev_local).astype(jnp.int32)
        live_mask = (jnp.arange(MAXT, dtype=jnp.int32)[None, :] < dev_counts[:, None]).reshape(NB_DEV * MAXT)
        picked = jnp.take(blocks, source_pos, axis=1) * live_mask.astype(blocks.dtype)[None, :, None]
        picked = picked.reshape(F, NB_DEV, MAXT, TB).astype(jnp.float32)
        weights = dev_tiles.reshape(NB_DEV, MAXT, TB, TB).astype(jnp.float32)
        summed = jnp.einsum('cbms,bmds->cbd', picked, weights)
        return summed / dev_counts.astype(jnp.float32)[None, :, None]
    per_device = lax.map(one_device, (counts.reshape(N_NODE, NB_DEV), src_owner.reshape(N_NODE, NB_DEV * MAXT), src_local.reshape(N_NODE, NB_DEV * MAXT), tiles.reshape(N_NODE, NB_DEV * MAXT, TB, TB)))
    aggregated = jnp.transpose(per_device, (1, 0, 2, 3)).reshape(F, NODES).astype(jnp.bfloat16)
    pre_act = jnp.dot(w_neigh.T, aggregated, preferred_element_type=jnp.float32) + self_part.astype(jnp.float32)
    hidden = jax.nn.silu(pre_act).astype(jnp.bfloat16)
    grad_pre = (cotangent.astype(jnp.float32) * silu_slope(pre_act)).astype(jnp.bfloat16)
    grad_scale = 1.0 / math.sqrt(NODES)
    grad_neigh = jnp.dot(grad_pre, aggregated.T, preferred_element_type=jnp.float32) * grad_scale
    return (hidden, grad_neigh)
```

```python
import math

import jax
import jax.numpy as jnp
from jax import lax
from jax.experimental import pallas as pl
from jax.experimental.pallas import tpu as pltpu
from jax.sharding import Mesh
from jax.sharding import PartitionSpec as P

MAXT = 3
CAP = 4
X, ZH, CORE, ZL, Y = 4, 4, 2, 8, 4
NEAR = 3 * CAP
FAR = CAP
VMEM = 48 * 1024 * 1024
f32, bf16 = jnp.float32, jnp.bfloat16


def vmem():
    return pl.BlockSpec(memory_space=pltpu.VMEM)


def smem():
    return pl.BlockSpec(memory_space=pltpu.SMEM)


def pack_kernel(first, each, stride, width, codes, *refs):
    held, out = refs[:-1], refs[-1]

    def one(i, carry):
        code = codes[(i // each) * stride + first + i % each]
        local = code % 16
        for j, ref in enumerate(held):

            @pl.when(code // 16 == j)
            def _(ref=ref):
                out[i] = ref[:, pl.ds(pl.multiple_of(local * width, width), width)]

        return carry

    lax.fori_loop(0, out.shape[0], one, 0, unroll=4)


def pack(codes, held, first, each, width):
    peers = X * CORE
    return pl.pallas_call(
        lambda *refs: pack_kernel(first, each, NEAR + FAR, width, *refs),
        out_shape=jax.ShapeDtypeStruct((peers * each, held[0].shape[0], width), held[0].dtype),
        in_specs=[smem()] + [vmem()] * len(held),
        out_specs=vmem(),
        compiler_params=pltpu.CompilerParams(vmem_limit_bytes=VMEM),
        cost_estimate=pl.CostEstimate(flops=0, bytes_accessed=4 << 20, transcendentals=0),
        name="pack",
    )(codes, *held)


def agg_kernel(pos, counts, near, far, tiles, out, acc):
    b = pl.program_id(0)
    count = counts[b]
    near_size = near.shape[0]
    for m in range(MAXT):
        p = pos[b * MAXT + m]

        def add(block, m=m):
            part = lax.dot_general(
                block, tiles[m], (((1,), (1,)), ((), ())), preferred_element_type=f32
            )
            if m == 0:
                acc[...] = part
            else:
                acc[...] += part

        @pl.when((m < count) & (p < near_size))
        def _():
            add(near[jnp.minimum(p, near_size - 1)])

        @pl.when((m < count) & (p >= near_size))
        def _():
            add(far[jnp.maximum(p - near_size, 0)])

    total = (acc[...] / count.astype(f32)).astype(out.dtype)
    half = out.shape[-1]
    for j in range(out.shape[0]):
        out[j] = total[:, j * half : (j + 1) * half]


def aggregate(pos, counts, near, far, tiles, node_cols):
    rows, width = near.shape[1:]
    blocks = counts.shape[0]
    per = width // node_cols
    return pl.pallas_call(
        agg_kernel,
        grid=(blocks,),
        out_shape=jax.ShapeDtypeStruct((blocks * per, rows, node_cols), bf16),
        in_specs=[
            smem(),
            smem(),
            vmem(),
            vmem(),
            pl.BlockSpec((MAXT, width, width), lambda b: (b, 0, 0)),
        ],
        out_specs=pl.BlockSpec((per, rows, node_cols), lambda b: (b, 0, 0)),
        scratch_shapes=[pltpu.VMEM((rows, width), f32)],
        compiler_params=pltpu.CompilerParams(vmem_limit_bytes=VMEM),
        cost_estimate=pl.CostEstimate(flops=2 * 48 * 24 * 65536, bytes_accessed=7 << 20, transcendentals=0),
        name="aggregate",
    )(pos, counts, near, far, tiles)


def dense_kernel(rows, w_t, self_part, cotangent, hidden, grad, gp):
    pre = jnp.dot(w_t[...], rows[...], preferred_element_type=f32) + self_part[...].astype(f32)
    sig = jax.nn.sigmoid(pre)
    hidden[...] = (pre * sig).astype(hidden.dtype)
    slope = sig * (1.0 + pre * (1.0 - sig))
    grad_pre = (cotangent[...].astype(f32) * slope).astype(bf16)
    piece = grad_pre.shape[0] // (ZL * Y)
    for zl in range(ZL):
        for y in range(Y):
            start = (zl * Y + y) * piece
            gp[y, zl] = grad_pre[start : start + piece]
    chunk = rows.shape[0] // (X * ZH * CORE)
    for y in range(Y):
        right = gp[y].reshape(ZL * piece, gp.shape[-1])
        part = lax.dot_general(
            rows[...], right, (((1,), (1,)), ((), ())), preferred_element_type=f32
        ).astype(grad.dtype)
        for x in range(X):
            for zh in range(ZH):
                for c in range(CORE):
                    start = ((x * ZH + zh) * CORE + c) * chunk
                    grad[(x * CORE + c) * Y + y, zh] = part[start : start + chunk]


def dense(rows, w_t, self_part, cotangent):
    hid, nodes = self_part.shape
    width = rows.shape[0]
    chunk, piece = width // (X * ZH * CORE), hid // (ZL * Y)
    return pl.pallas_call(
        dense_kernel,
        out_shape=(
            jax.ShapeDtypeStruct((hid, nodes), bf16),
            jax.ShapeDtypeStruct((X * CORE * Y, ZH, chunk, ZL * piece), bf16),
        ),
        in_specs=[vmem()] * 4,
        out_specs=(vmem(), vmem()),
        scratch_shapes=[pltpu.VMEM((Y, ZL, piece, nodes), bf16)],
        compiler_params=pltpu.CompilerParams(vmem_limit_bytes=VMEM),
        cost_estimate=pl.CostEstimate(flops=4 * 512 * 768 * 128, bytes_accessed=2 << 20, transcendentals=512 * 128),
        name="dense",
    )(rows, w_t, self_part, cotangent)


def ring(value, step):
    return lax.ppermute(value, "zh", [(i, (i + step) % ZH) for i in range(ZH)])


def plan(counts, owners, local):
    me = lax.axis_index("zh")
    slots = owners.shape[0]
    column = (owners // (ZH * CORE)) * CORE + owners % CORE
    apart = (owners // CORE + ZH - me) % ZH
    far = apart == 2
    group = column + jnp.where(far, X * CORE, 0)
    same = group[:, None] == group[None, :]
    s = jnp.arange(slots, dtype=jnp.int32)
    rank = jnp.sum((same & (s[None, :] < s[:, None])).astype(jnp.int32), axis=1)
    pos = jnp.where(far, X * CORE * NEAR + column * FAR + rank, column * NEAR + rank)
    code = local + jnp.where(apart == 1, 16, jnp.where(apart == 3, 32, 0))
    place = column * (NEAR + FAR) + rank + jnp.where(far, NEAR, 0)
    asked = X * CORE * (NEAR + FAR)
    hit = place[:, None] == jnp.arange(asked, dtype=jnp.int32)[None, :]
    ask = jnp.sum(jnp.where(hit, code[:, None], 0), axis=0)
    return pos, ask


def per_device(features, counts, src_owner, src_local, tiles, w_neigh, self_part, cotangent):
    rows, cols = features.shape
    blocks = counts.shape[0]
    width = tiles.shape[1]
    node_cols = self_part.shape[1]
    peers = X * CORE
    up = ring(features, -1)
    down = ring(features, 1)
    pos, ask = plan(counts, src_owner[:, 0], src_local)
    codes = lax.all_to_all(ask.reshape(peers, -1), ("x", "c"), 0, 0).reshape(-1)
    w_t = w_neigh.T
    half = cols // 2
    across = jnp.concatenate([ring(up[:, :half], -1), ring(down[:, half:], 1)], axis=1)
    near = pack(codes, (features, up, down), 0, NEAR, width)
    near = lax.all_to_all(
        near.reshape(peers, NEAR, rows, width), ("x", "c"), 0, 0
    ).reshape(peers * NEAR, rows, width)
    far = pack(codes, (across,), NEAR, FAR, width)
    far = lax.all_to_all(
        far.reshape(peers, FAR, rows, width), ("x", "c"), 0, 0
    ).reshape(peers * FAR, rows, width)
    aggregated = aggregate(pos, counts, near, far, tiles, node_cols)
    node_rows = lax.all_to_all(aggregated, ("zl", "y"), 0, 0).reshape(-1, node_cols)
    hidden, grad = dense(node_rows, w_t, self_part, cotangent)
    grad = lax.all_to_all(grad, ("x", "c", "y"), 0, 0)
    grad = jnp.sum(grad.astype(f32), axis=0)
    me = lax.axis_index("zh")
    total = lax.dynamic_index_in_dim(grad, me, 0, keepdims=False)
    for step in (1, 2, 3):
        total = total + ring(lax.dynamic_index_in_dim(grad, (me + step) % ZH, 0, keepdims=False), step)
    total = total.T.reshape(ZL, -1, rows)
    total = lax.all_to_all(total, "zl", 0, 0)
    grad_scale = 1.0 / math.sqrt(cols * X * ZH * CORE)
    return hidden, jnp.sum(total, axis=0) * grad_scale


def solution(mesh):
    fine = Mesh(mesh.devices.reshape(X, ZH, CORE, ZL, Y), ("x", "zh", "c", "zl", "y"))
    node, feat = ("x", "zh", "c"), ("zl", "y")
    return jax.shard_map(
        per_device,
        mesh=fine,
        in_specs=(
            P(feat, node),
            P(node),
            P(node, None),
            P(node),
            P(node, None, None),
            P(),
            P(None, node + feat),
            P(None, node + feat),
        ),
        out_specs=(P(None, node + feat), P(feat, node)),
        check_vma=False,
    )
```

```python
import math

import jax
import jax.numpy as jnp
from jax import lax
from jax.experimental import pallas as pl
from jax.experimental.pallas import tpu as pltpu
from jax.sharding import Mesh
from jax.sharding import PartitionSpec as P

MAXT = 3
CAP = 4
X, ZH, CORE, ZL, Y = 4, 4, 2, 8, 4
EACH = ZH * CAP
VMEM = 48 * 1024 * 1024
f32, bf16 = jnp.float32, jnp.bfloat16


def vmem():
    return pl.BlockSpec(memory_space=pltpu.VMEM)


def smem():
    return pl.BlockSpec(memory_space=pltpu.SMEM)


def pack_kernel(width, codes, *refs):
    held, out = refs[:-1], refs[-1]

    def one(i, carry):
        code = codes[i]
        local = code % 16
        for j, ref in enumerate(held):

            @pl.when(code // 16 == j)
            def _(ref=ref):
                out[i] = ref[:, pl.ds(pl.multiple_of(local * width, width), width)]

        return carry

    lax.fori_loop(0, out.shape[0], one, 0, unroll=4)


def pack(codes, held, width):
    return pl.pallas_call(
        lambda *refs: pack_kernel(width, *refs),
        out_shape=jax.ShapeDtypeStruct((codes.shape[0], held[0].shape[0], width), held[0].dtype),
        in_specs=[smem()] + [vmem()] * len(held),
        out_specs=vmem(),
        compiler_params=pltpu.CompilerParams(vmem_limit_bytes=VMEM),
        cost_estimate=pl.CostEstimate(flops=0, bytes_accessed=2 << 20, transcendentals=0),
        name="pack",
    )(codes, *held)


def agg_kernel(pos, counts, blocks, tiles, out):
    half = out.shape[-1]
    per = tiles.shape[1] // half

    def one(b, carry):
        count = counts[b]
        total = None
        for m in range(MAXT):
            block = blocks[pos[b * MAXT + m]]
            block = jnp.where(m < count, block, jnp.zeros_like(block))
            part = lax.dot_general(
                block, tiles[b * MAXT + m], (((1,), (1,)), ((), ())), preferred_element_type=f32
            )
            total = part if m == 0 else total + part
        total = (total / count.astype(f32)).astype(out.dtype)
        for j in range(per):
            out[b * per + j] = total[:, j * half : (j + 1) * half]
        return carry

    lax.fori_loop(0, counts.shape[0], one, 0, unroll=8)


def aggregate(pos, counts, blocks, tiles, node_cols):
    rows, width = blocks.shape[1:]
    return pl.pallas_call(
        agg_kernel,
        out_shape=jax.ShapeDtypeStruct((counts.shape[0] * width // node_cols, rows, node_cols), bf16),
        in_specs=[smem(), smem(), vmem(), vmem()],
        out_specs=vmem(),
        compiler_params=pltpu.CompilerParams(vmem_limit_bytes=VMEM),
        cost_estimate=pl.CostEstimate(flops=2 * 48 * 24 * 65536, bytes_accessed=7 << 20, transcendentals=0),
        name="aggregate",
    )(pos, counts, blocks, tiles)


def dense_kernel(rows, w_t, self_part, cotangent, hidden, grad, gp):
    pre = jnp.dot(w_t[...], rows[...], preferred_element_type=f32) + self_part[...].astype(f32)
    sig = jax.nn.sigmoid(pre)
    hidden[...] = (pre * sig).astype(hidden.dtype)
    slope = sig * (1.0 + pre * (1.0 - sig))
    grad_pre = (cotangent[...].astype(f32) * slope).astype(bf16)
    piece = grad_pre.shape[0] // (ZL * Y)
    for zl in range(ZL):
        for y in range(Y):
            start = (zl * Y + y) * piece
            gp[y, zl] = grad_pre[start : start + piece]
    chunk = rows.shape[0] // (X * ZH * CORE)
    for y in range(Y):
        right = gp[y].reshape(ZL * piece, gp.shape[-1])
        part = lax.dot_general(
            rows[...], right, (((1,), (1,)), ((), ())), preferred_element_type=f32
        ).astype(grad.dtype)
        for x in range(X):
            for zh in range(ZH):
                for c in range(CORE):
                    start = ((x * ZH + zh) * CORE + c) * chunk
                    grad[(x * CORE + c) * Y + y, zh] = part[start : start + chunk]


def dense(rows, w_t, self_part, cotangent):
    hid, nodes = self_part.shape
    width = rows.shape[0]
    chunk, piece = width // (X * ZH * CORE), hid // (ZL * Y)
    return pl.pallas_call(
        dense_kernel,
        out_shape=(
            jax.ShapeDtypeStruct((hid, nodes), bf16),
            jax.ShapeDtypeStruct((X * CORE * Y, ZH, chunk, ZL * piece), bf16),
        ),
        in_specs=[vmem()] * 4,
        out_specs=(vmem(), vmem()),
        scratch_shapes=[pltpu.VMEM((Y, ZL, piece, nodes), bf16)],
        compiler_params=pltpu.CompilerParams(vmem_limit_bytes=VMEM),
        cost_estimate=pl.CostEstimate(flops=4 * 512 * 768 * 128, bytes_accessed=2 << 20, transcendentals=512 * 128),
        name="dense",
    )(rows, w_t, self_part, cotangent)


def onward(value, step):
    pairs = []
    for z in range(ZH):
        pairs.append((z * CORE, (z + step) % ZH * CORE))
        pairs.append((z * CORE + 1, (z - step) % ZH * CORE + 1))
    return lax.ppermute(value, ("zh", "c"), pairs)


def plan(owners, local):
    me = lax.axis_index("zh")
    slots = owners.shape[0]
    core = owners % CORE
    apart = (me + ZH - owners // CORE % ZH) % ZH
    apart = jnp.where(core == 0, apart, (ZH - apart) % ZH)
    held = jnp.where(apart == 2, 3, jnp.where(apart == 3, 2, apart))
    column = (owners // (ZH * CORE)) * CORE + core
    s = jnp.arange(slots, dtype=jnp.int32)
    earlier = (column[:, None] == column[None, :]) & (s[None, :] < s[:, None])
    pos = column * EACH + jnp.sum(earlier.astype(jnp.int32), axis=1)
    hit = pos[:, None] == jnp.arange(X * CORE * EACH, dtype=jnp.int32)[None, :]
    return pos, jnp.sum(jnp.where(hit, (held * 16 + local)[:, None], 0), axis=0)


def per_device(features, counts, src_owner, src_local, tiles, w_neigh, self_part, cotangent):
    rows, cols = features.shape
    width = tiles.shape[1]
    node_cols = self_part.shape[1]
    first = onward(features, 1)
    second = onward(features, -1)
    pos, ask = plan(src_owner[:, 0], src_local)
    codes = lax.all_to_all(ask.reshape(X * CORE, EACH), ("x", "c"), 0, 0).reshape(-1)
    codes, first = lax.optimization_barrier((codes, first))
    third = onward(first, 1)
    blocks = pack(codes, (features, first, second, third), width)
    blocks = lax.all_to_all(blocks.reshape(X * CORE, EACH, rows, width), ("x", "c"), 0, 0)
    aggregated = aggregate(pos, counts, blocks.reshape(-1, rows, width), tiles, node_cols)
    node_rows = lax.all_to_all(aggregated, ("zl", "y"), 0, 0).reshape(-1, node_cols)
    hidden, grad = dense(node_rows, w_neigh.T, self_part, cotangent)
    grad = lax.all_to_all(grad, ("x", "c", "y"), 0, 0)
    grad = jnp.sum(grad.astype(f32), axis=0)
    grad = jnp.sum(lax.all_to_all(grad, "zh", 0, 0), axis=0)
    grad = lax.all_to_all(grad.T.reshape(ZL, -1, rows), "zl", 0, 0)
    grad_scale = 1.0 / math.sqrt(cols * X * ZH * CORE)
    return hidden, jnp.sum(grad, axis=0) * grad_scale


def solution(mesh):
    fine = Mesh(mesh.devices.reshape(X, ZH, CORE, ZL, Y), ("x", "zh", "c", "zl", "y"))
    node, feat = ("x", "zh", "c"), ("zl", "y")
    return jax.shard_map(
        per_device,
        mesh=fine,
        in_specs=(
            P(feat, node),
            P(node),
            P(node, None),
            P(node),
            P(node, None, None),
            P(),
            P(None, node + feat),
            P(None, node + feat),
        ),
        out_specs=(P(None, node + feat), P(feat, node)),
        check_vma=False,
    )
```

```python
import math

import jax
import jax.numpy as jnp
from jax import lax
from jax.experimental import pallas as pl
from jax.experimental.pallas import tpu as pltpu
from jax.sharding import Mesh
from jax.sharding import PartitionSpec as P

MAXT = 3
CAP = 4
X, ZH, CORE, ZL, Y = 4, 4, 2, 8, 4
EACH = 2 * CAP
VMEM = 48 * 1024 * 1024
f32, bf16 = jnp.float32, jnp.bfloat16


def vmem():
    return pl.BlockSpec(memory_space=pltpu.VMEM)


def smem():
    return pl.BlockSpec(memory_space=pltpu.SMEM)


def pack_kernel(first, width, codes, *refs):
    held, out = refs[:-1], refs[-1]
    peers, each = out.shape[0], out.shape[1]
    asked = codes.shape[0] // peers

    def one(d, carry):
        for k in range(each):
            code = codes[d * asked + first + k]
            place = pl.ds(pl.multiple_of(code % 16 * width, width), width)
            out[d, k] = jnp.where(code < 16, held[0][:, place], held[1][:, place])
        return carry

    lax.fori_loop(0, peers, one, 0, unroll=2)


def pack(codes, held, first, width):
    return pl.pallas_call(
        lambda *refs: pack_kernel(first, width, *refs),
        out_shape=jax.ShapeDtypeStruct((X * CORE, EACH, held[0].shape[0], width), held[0].dtype),
        in_specs=[smem()] + [vmem()] * len(held),
        out_specs=vmem(),
        compiler_params=pltpu.CompilerParams(vmem_limit_bytes=VMEM),
        cost_estimate=pl.CostEstimate(flops=0, bytes_accessed=2 << 20, transcendentals=0),
        name="pack",
    )(codes, *held)


def agg_kernel(pos, counts, early, late, tiles, out):
    early_size = early.shape[0]
    half = out.shape[-1]
    per = tiles.shape[1] // half

    def one(b, carry):
        count = counts[b]
        total = None
        for m in range(MAXT):
            p = pos[b * MAXT + m]
            block = jnp.where(
                p < early_size,
                early[jnp.minimum(p, early_size - 1)],
                late[jnp.maximum(p - early_size, 0)],
            )
            block = jnp.where(m < count, block, jnp.zeros_like(block))
            part = lax.dot_general(
                block, tiles[b * MAXT + m], (((1,), (1,)), ((), ())), preferred_element_type=f32
            )
            total = part if m == 0 else total + part
        total = (total / count.astype(f32)).astype(out.dtype)
        for j in range(per):
            out[b * per + j] = total[:, j * half : (j + 1) * half]
        return carry

    lax.fori_loop(0, counts.shape[0], one, 0, unroll=8)


def aggregate(pos, counts, early, late, tiles, node_cols):
    rows, width = early.shape[1:]
    return pl.pallas_call(
        agg_kernel,
        out_shape=jax.ShapeDtypeStruct((counts.shape[0] * width // node_cols, rows, node_cols), bf16),
        in_specs=[smem(), smem(), vmem(), vmem(), vmem()],
        out_specs=vmem(),
        compiler_params=pltpu.CompilerParams(vmem_limit_bytes=VMEM),
        cost_estimate=pl.CostEstimate(flops=2 * 48 * 24 * 65536, bytes_accessed=7 << 20, transcendentals=0),
        name="aggregate",
    )(pos, counts, early, late, tiles)


def dense_kernel(rows, w_t, self_part, cotangent, hidden, grad, gp):
    pre = jnp.dot(w_t[...], rows[...], preferred_element_type=f32) + self_part[...].astype(f32)
    sig = jax.nn.sigmoid(pre)
    hidden[...] = (pre * sig).astype(hidden.dtype)
    slope = sig * (1.0 + pre * (1.0 - sig))
    grad_pre = (cotangent[...].astype(f32) * slope).astype(bf16)
    piece = grad_pre.shape[0] // (ZL * Y)
    for zl in range(ZL):
        for y in range(Y):
            start = (zl * Y + y) * piece
            gp[y, zl] = grad_pre[start : start + piece]
    chunk = rows.shape[0] // (X * ZH * CORE)
    for y in range(Y):
        right = gp[y].reshape(ZL * piece, gp.shape[-1])
        part = lax.dot_general(
            rows[...], right, (((1,), (1,)), ((), ())), preferred_element_type=f32
        ).astype(grad.dtype)
        for x in range(X):
            for zh in range(ZH):
                for c in range(CORE):
                    start = ((x * ZH + zh) * CORE + c) * chunk
                    grad[(x * CORE + c) * Y + y, zh] = part[start : start + chunk]


def fold_kernel(parts, out):
    total = jnp.sum(parts[...].astype(f32), axis=0)
    total = jnp.concatenate([total[z] for z in range(total.shape[0])], axis=0)
    out[...] = total.T.reshape(out.shape)


def fold(parts):
    chunk, lanes = parts.shape[2:]
    return pl.pallas_call(
        fold_kernel,
        out_shape=jax.ShapeDtypeStruct((ZL, lanes // ZL, ZH * chunk), f32),
        in_specs=[vmem()],
        out_specs=vmem(),
        compiler_params=pltpu.CompilerParams(vmem_limit_bytes=VMEM),
        cost_estimate=pl.CostEstimate(flops=32 * 96 * 128, bytes_accessed=1 << 20, transcendentals=0),
        name="fold",
    )(parts)


def dense(rows, w_t, self_part, cotangent):
    hid, nodes = self_part.shape
    width = rows.shape[0]
    chunk, piece = width // (X * ZH * CORE), hid // (ZL * Y)
    return pl.pallas_call(
        dense_kernel,
        out_shape=(
            jax.ShapeDtypeStruct((hid, nodes), bf16),
            jax.ShapeDtypeStruct((X * CORE * Y, ZH, chunk, ZL * piece), bf16),
        ),
        in_specs=[vmem()] * 4,
        out_specs=(vmem(), vmem()),
        scratch_shapes=[pltpu.VMEM((Y, ZL, piece, nodes), bf16)],
        compiler_params=pltpu.CompilerParams(vmem_limit_bytes=VMEM),
        cost_estimate=pl.CostEstimate(flops=4 * 512 * 768 * 128, bytes_accessed=2 << 20, transcendentals=512 * 128),
        name="dense",
    )(rows, w_t, self_part, cotangent)


def onward(value, step):
    pairs = []
    for z in range(ZH):
        pairs.append((z * CORE, (z + step) % ZH * CORE))
        pairs.append((z * CORE + 1, (z - step) % ZH * CORE + 1))
    return lax.ppermute(value, ("zh", "c"), pairs)


def plan(owners, local):
    me = lax.axis_index("zh")
    slots = owners.shape[0]
    core = owners % CORE
    apart = (me + ZH - owners // CORE % ZH) % ZH
    apart = jnp.where(core == 0, apart, (ZH - apart) % ZH)
    second = apart > 1
    held = (apart == 1) | (apart == 2)
    column = (owners // (ZH * CORE)) * CORE + core
    group = column + jnp.where(second, X * CORE, 0)
    s = jnp.arange(slots, dtype=jnp.int32)
    earlier = (group[:, None] == group[None, :]) & (s[None, :] < s[:, None])
    rank = jnp.sum(earlier.astype(jnp.int32), axis=1)
    place = column * 2 * EACH + jnp.where(second, EACH, 0) + rank
    hit = place[:, None] == jnp.arange(X * CORE * 2 * EACH, dtype=jnp.int32)[None, :]
    ask = jnp.sum(jnp.where(hit, (held.astype(jnp.int32) * 16 + local)[:, None], 0), axis=0)
    return group * EACH + rank, ask


def exchange(packed):
    return lax.all_to_all(packed, ("x", "c"), 0, 0).reshape((-1,) + packed.shape[2:])


def per_device(features, counts, src_owner, src_local, tiles, w_neigh, self_part, cotangent):
    rows, cols = features.shape
    width = tiles.shape[1]
    node_cols = self_part.shape[1]
    first = onward(features, 1)
    pos, ask = plan(src_owner[:, 0], src_local)
    codes = lax.all_to_all(ask.reshape(X * CORE, -1), ("x", "c"), 0, 0).reshape(-1)
    codes, first, again = lax.optimization_barrier((codes, first, features))
    third = onward(first, 1)
    second = onward(again, -1)
    early = exchange(pack(codes, (features, first), 0, width))
    early, second, third = lax.optimization_barrier((early, second, third))
    late = exchange(pack(codes, (second, third), EACH, width))
    aggregated = aggregate(pos, counts, early, late, tiles, node_cols)
    node_rows = lax.all_to_all(aggregated, ("zl", "y"), 0, 0).reshape(-1, node_cols)
    hidden, grad = dense(node_rows, w_neigh.T, self_part, cotangent)
    grad = fold(lax.all_to_all(grad, ("x", "c", "y"), 0, 0))
    grad = jnp.sum(lax.all_to_all(grad, "zl", 0, 0), axis=0)
    grad = jnp.transpose(grad.reshape(-1, ZH, rows), (1, 0, 2))
    grad_scale = 1.0 / math.sqrt(cols * X * ZH * CORE)
    return hidden, jnp.sum(lax.all_to_all(grad, "zh", 0, 0), axis=0) * grad_scale


def solution(mesh):
    fine = Mesh(mesh.devices.reshape(X, ZH, CORE, ZL, Y), ("x", "zh", "c", "zl", "y"))
    node, feat = ("x", "zh", "c"), ("zl", "y")
    return jax.shard_map(
        per_device,
        mesh=fine,
        in_specs=(
            P(feat, node),
            P(node),
            P(node, None),
            P(node),
            P(node, None, None),
            P(),
            P(None, node + feat),
            P(None, node + feat),
        ),
        out_specs=(P(None, node + feat), P(feat, node)),
        check_vma=False,
    )
```

```python
import math

import jax
import jax.numpy as jnp
from jax import lax
from jax.experimental import pallas as pl
from jax.experimental.pallas import tpu as pltpu
from jax.sharding import Mesh
from jax.sharding import PartitionSpec as P

MAXT = 3
CAP = 4
X, ZH, CORE, ZL, Y = 4, 4, 2, 8, 4
EACH = 2 * CAP
VMEM = 16 * 1024 * 1024
f32, bf16 = jnp.float32, jnp.bfloat16


def vmem():
    return pl.BlockSpec(memory_space=pltpu.VMEM)


def smem():
    return pl.BlockSpec(memory_space=pltpu.SMEM)


def pack_kernel(first, width, codes, *refs):
    held, out = refs[:-1], refs[-1]
    stacked = len(held) == 1
    peers, each = out.shape[0], out.shape[1]
    asked = codes.shape[0] // peers

    def one(d, carry):
        for k in range(each):
            code = codes[d * asked + first + k]
            place = pl.ds(pl.multiple_of(code % 16 * width, width), width)
            if stacked:
                out[d, k] = held[0][code // 16, :, place]
            else:
                out[d, k] = jnp.where(code < 16, held[0][:, place], held[1][:, place])
        return carry

    lax.fori_loop(0, peers, one, 0, unroll=2)


def pack(codes, held, first, width):
    return pl.pallas_call(
        lambda *refs: pack_kernel(first, width, *refs),
        out_shape=jax.ShapeDtypeStruct((X * CORE, EACH, held[0].shape[-2], width), held[0].dtype),
        in_specs=[smem()] + [vmem()] * len(held),
        out_specs=vmem(),
        compiler_params=pltpu.CompilerParams(vmem_limit_bytes=VMEM),
        cost_estimate=pl.CostEstimate(flops=0, bytes_accessed=2 << 20, transcendentals=0),
        name="pack",
    )(codes, *held)


def agg_kernel(pos, counts, early, late, tiles_in, out, tiles, arrived):
    early_size = early.shape[0]
    half = out.shape[-1]
    per = tiles.shape[1] // half

    def fetch(b):
        own = pl.ds(b * MAXT, MAXT)
        return pltpu.make_async_copy(tiles_in.at[own], tiles.at[own], arrived.at[b])

    for b in range(counts.shape[0]):
        fetch(b).start()

    def one(b, carry):
        fetch(b).wait()
        count = counts[b]
        total = None
        for m in range(MAXT):
            p = pos[b * MAXT + m]
            block = jnp.where(
                p < early_size,
                early[jnp.minimum(p, early_size - 1)],
                late[jnp.maximum(p - early_size, 0)],
            )
            block = jnp.where(m < count, block, jnp.zeros_like(block))
            part = lax.dot_general(
                block, tiles[b * MAXT + m], (((1,), (1,)), ((), ())), preferred_element_type=f32
            )
            total = part if m == 0 else total + part
        total = (total / count.astype(f32)).astype(out.dtype)
        for j in range(per):
            out[b * per + j] = total[:, j * half : (j + 1) * half]
        return carry

    lax.fori_loop(0, counts.shape[0], one, 0, unroll=8)


def aggregate(pos, counts, early, late, tiles, node_cols):
    rows, width = early.shape[1:]
    return pl.pallas_call(
        agg_kernel,
        out_shape=jax.ShapeDtypeStruct((counts.shape[0] * width // node_cols, rows, node_cols), bf16),
        in_specs=[smem(), smem(), vmem(), vmem(), pl.BlockSpec(memory_space=pltpu.HBM)],
        out_specs=vmem(),
        scratch_shapes=[pltpu.VMEM(tiles.shape, tiles.dtype), pltpu.SemaphoreType.DMA(counts.shape)],
        compiler_params=pltpu.CompilerParams(vmem_limit_bytes=50 * 1024 * 1024),
        cost_estimate=pl.CostEstimate(flops=2 * 48 * 24 * 65536, bytes_accessed=7 << 20, transcendentals=0),
        name="aggregate",
    )(pos, counts, early, late, tiles)


def dense_kernel(rows, w_t, self_part, cotangent, hidden, grad, gp):
    pre = jnp.dot(w_t[...], rows[...], preferred_element_type=f32) + self_part[...].astype(f32)
    sig = jax.nn.sigmoid(pre)
    hidden[...] = (pre * sig).astype(hidden.dtype)
    slope = sig * (1.0 + pre * (1.0 - sig))
    grad_pre = (cotangent[...].astype(f32) * slope).astype(bf16)
    piece = grad_pre.shape[0] // (ZL * Y)
    for zl in range(ZL):
        for y in range(Y):
            start = (zl * Y + y) * piece
            gp[y, zl] = grad_pre[start : start + piece]
    chunk = rows.shape[0] // (X * ZH * CORE)
    for y in range(Y):
        right = gp[y].reshape(ZL * piece, gp.shape[-1])
        part = lax.dot_general(
            rows[...], right, (((1,), (1,)), ((), ())), preferred_element_type=f32
        ).astype(grad.dtype)
        for x in range(X):
            for zh in range(ZH):
                for c in range(CORE):
                    start = ((x * ZH + zh) * CORE + c) * chunk
                    grad[(x * CORE + c) * Y + y, zh] = part[start : start + chunk]


def fold_kernel(parts, out):
    total = jnp.sum(parts[...].astype(f32), axis=0)
    total = jnp.concatenate([total[z] for z in range(total.shape[0])], axis=0)
    out[...] = total.T.reshape(out.shape)


def fold(parts):
    chunk, lanes = parts.shape[2:]
    return pl.pallas_call(
        fold_kernel,
        out_shape=jax.ShapeDtypeStruct((ZL, lanes // ZL, ZH * chunk), f32),
        in_specs=[vmem()],
        out_specs=vmem(),
        compiler_params=pltpu.CompilerParams(vmem_limit_bytes=VMEM),
        cost_estimate=pl.CostEstimate(flops=32 * 96 * 128, bytes_accessed=1 << 20, transcendentals=0),
        name="fold",
    )(parts)


def dense(rows, w_t, self_part, cotangent):
    hid, nodes = self_part.shape
    width = rows.shape[0]
    chunk, piece = width // (X * ZH * CORE), hid // (ZL * Y)
    return pl.pallas_call(
        dense_kernel,
        out_shape=(
            jax.ShapeDtypeStruct((hid, nodes), bf16),
            jax.ShapeDtypeStruct((X * CORE * Y, ZH, chunk, ZL * piece), bf16),
        ),
        in_specs=[vmem()] * 4,
        out_specs=(vmem(), vmem()),
        scratch_shapes=[pltpu.VMEM((Y, ZL, piece, nodes), bf16)],
        compiler_params=pltpu.CompilerParams(vmem_limit_bytes=VMEM),
        cost_estimate=pl.CostEstimate(flops=4 * 512 * 768 * 128, bytes_accessed=2 << 20, transcendentals=512 * 128),
        name="dense",
    )(rows, w_t, self_part, cotangent)


def onward(value):
    pairs = []
    for z in range(ZH):
        pairs.append((z * CORE, (z + 1) % ZH * CORE))
        pairs.append((z * CORE + 1, (z - 1) % ZH * CORE + 1))
    return lax.ppermute(value, ("zh", "c"), pairs)


def plan(owners, local):
    me = lax.axis_index("zh")
    slots = owners.shape[0]
    core = owners % CORE
    apart = (owners // CORE + ZH - me) % ZH
    server = jnp.where(apart == 3, 0, jnp.where(apart == 1, 1, core))
    second = (apart == 2) | ((apart % 2 == 1) & (server != core))
    held = (apart == 2) | ((apart % 2 == 1) & (server == core))
    column = (owners // (ZH * CORE)) * CORE + server
    group = column + jnp.where(second, X * CORE, 0)
    s = jnp.arange(slots, dtype=jnp.int32)
    earlier = (group[:, None] == group[None, :]) & (s[None, :] < s[:, None])
    rank = jnp.sum(earlier.astype(jnp.int32), axis=1)
    place = column * 2 * EACH + jnp.where(second, EACH, 0) + rank
    hit = place[:, None] == jnp.arange(X * CORE * 2 * EACH, dtype=jnp.int32)[None, :]
    ask = jnp.sum(jnp.where(hit, (held.astype(jnp.int32) * 16 + local)[:, None], 0), axis=0)
    return group * EACH + rank, ask


def exchange(packed):
    return lax.all_to_all(packed, ("x", "c"), 0, 0).reshape((-1,) + packed.shape[2:])


def per_device(features, counts, src_owner, src_local, tiles, w_neigh, self_part, cotangent):
    rows, cols = features.shape
    width = tiles.shape[1]
    node_cols = self_part.shape[1]
    first = onward(features)
    other = lax.ppermute(features, "c", [(0, 1), (1, 0)])
    pos, ask = plan(src_owner[:, 0], src_local)
    ask, other = lax.optimization_barrier((ask, other))
    codes = lax.all_to_all(ask.reshape(X * CORE, -1), ("x", "c"), 0, 0).reshape(-1)
    codes, first, other = lax.optimization_barrier((codes, first, other))
    late = onward(jnp.concatenate([other[None], first[None]]))
    early = lax.cond(
        counts[0] > 0,
        lambda: exchange(pack(codes, (features, first), 0, width)),
        lambda: jnp.zeros((X * CORE * EACH, rows, width), bf16),
    )
    early, late = lax.optimization_barrier((early, late))
    late = exchange(pack(codes, (late,), EACH, width))
    aggregated = aggregate(pos, counts, early, late, tiles, node_cols)
    node_rows = lax.all_to_all(aggregated, ("zl", "y"), 0, 0).reshape(-1, node_cols)
    hidden, grad = dense(node_rows, w_neigh.T, self_part, cotangent)
    grad = fold(lax.all_to_all(grad, ("x", "c", "y"), 0, 0))
    grad = jnp.sum(lax.all_to_all(grad, "zl", 0, 0), axis=0)
    grad = jnp.transpose(grad.reshape(-1, ZH, rows), (1, 0, 2))
    grad_scale = 1.0 / math.sqrt(cols * X * ZH * CORE)
    return hidden, jnp.sum(lax.all_to_all(grad, "zh", 0, 0), axis=0) * grad_scale


def solution(mesh):
    fine = Mesh(mesh.devices.reshape(X, ZH, CORE, ZL, Y), ("x", "zh", "c", "zl", "y"))
    node, feat = ("x", "zh", "c"), ("zl", "y")
    return jax.shard_map(
        per_device,
        mesh=fine,
        in_specs=(
            P(feat, node),
            P(node),
            P(node, None),
            P(node),
            P(node, None, None),
            P(),
            P(None, node + feat),
            P(None, node + feat),
        ),
        out_specs=(P(None, node + feat), P(feat, node)),
        check_vma=False,
    )
```

```python
import math

import jax
import jax.numpy as jnp
from jax import lax
from jax.experimental import pallas as pl
from jax.experimental.pallas import tpu as pltpu
from jax.sharding import Mesh
from jax.sharding import PartitionSpec as P

MAXT = 3
CAP = 4
X, ZH, CORE, ZL, Y = 4, 4, 2, 8, 4
EACH = 2 * CAP
GROUPS = 4
VMEM = 16 * 1024 * 1024
f32, bf16 = jnp.float32, jnp.bfloat16


def vmem():
    return pl.BlockSpec(memory_space=pltpu.VMEM)


def smem():
    return pl.BlockSpec(memory_space=pltpu.SMEM)


def pack_kernel(first, width, codes, *refs):
    held, out = refs[:-1], refs[-1]
    stacked = len(held) == 1
    peers, each = out.shape[0], out.shape[1]
    asked = codes.shape[0] // peers

    def one(d, carry):
        for k in range(each):
            code = codes[d * asked + first + k]
            place = pl.ds(pl.multiple_of(code % 16 * width, width), width)
            if stacked:
                out[d, k] = held[0][code // 16, :, place]
            else:
                out[d, k] = jnp.where(code < 16, held[0][:, place], held[1][:, place])
        return carry

    lax.fori_loop(0, peers, one, 0, unroll=2)


def pack(codes, held, first, width):
    return pl.pallas_call(
        lambda *refs: pack_kernel(first, width, *refs),
        out_shape=jax.ShapeDtypeStruct((X * CORE, EACH, held[0].shape[-2], width), held[0].dtype),
        in_specs=[smem()] + [vmem()] * len(held),
        out_specs=vmem(),
        compiler_params=pltpu.CompilerParams(vmem_limit_bytes=VMEM),
        cost_estimate=pl.CostEstimate(flops=0, bytes_accessed=2 << 20, transcendentals=0),
        name="pack",
    )(codes, *held)


def agg_kernel(pos, counts, early, late, tiles_in, out, tiles, arrived):
    early_size = early.shape[0]
    half = out.shape[-1]
    per = tiles.shape[1] // half
    groups = arrived.shape[0]
    size = counts.shape[0] // groups

    def fetch(g):
        own = pl.ds(g * size * MAXT, size * MAXT)
        return pltpu.make_async_copy(tiles_in.at[own], tiles.at[own], arrived.at[g])

    for g in range(groups):
        fetch(g).start()

    def one(g, carry):
        fetch(g).wait()
        for b in [g * size + i for i in range(size)]:
            count = counts[b]
            total = None
            for m in range(MAXT):
                p = pos[b * MAXT + m]
                block = jnp.where(
                    p < early_size,
                    early[jnp.minimum(p, early_size - 1)],
                    late[jnp.maximum(p - early_size, 0)],
                )
                block = jnp.where(m < count, block, jnp.zeros_like(block))
                part = lax.dot_general(
                    block, tiles[b * MAXT + m], (((1,), (1,)), ((), ())), preferred_element_type=f32
                )
                total = part if m == 0 else total + part
            total = (total / count.astype(f32)).astype(out.dtype)
            for j in range(per):
                out[b * per + j] = total[:, j * half : (j + 1) * half]
        return carry

    lax.fori_loop(0, groups, one, 0)


def aggregate(pos, counts, early, late, tiles, node_cols):
    rows, width = early.shape[1:]
    return pl.pallas_call(
        agg_kernel,
        out_shape=jax.ShapeDtypeStruct((counts.shape[0] * width // node_cols, rows, node_cols), bf16),
        in_specs=[smem(), smem(), vmem(), vmem(), pl.BlockSpec(memory_space=pltpu.HBM)],
        out_specs=vmem(),
        scratch_shapes=[pltpu.VMEM(tiles.shape, tiles.dtype), pltpu.SemaphoreType.DMA((GROUPS,))],
        compiler_params=pltpu.CompilerParams(vmem_limit_bytes=50 * 1024 * 1024),
        cost_estimate=pl.CostEstimate(flops=2 * 48 * 24 * 65536, bytes_accessed=7 << 20, transcendentals=0),
        name="aggregate",
    )(pos, counts, early, late, tiles)


def dense_kernel(rows, w_t, self_part, cotangent, hidden, grad, gp):
    pre = jnp.dot(w_t[...], rows[...], preferred_element_type=f32) + self_part[...].astype(f32)
    sig = jax.nn.sigmoid(pre)
    hidden[...] = (pre * sig).astype(hidden.dtype)
    slope = sig * (1.0 + pre * (1.0 - sig))
    grad_pre = (cotangent[...].astype(f32) * slope).astype(bf16)
    piece = grad_pre.shape[0] // (ZL * Y)
    for zl in range(ZL):
        for y in range(Y):
            start = (zl * Y + y) * piece
            gp[y, zl] = grad_pre[start : start + piece]
    chunk = rows.shape[0] // (X * ZH * CORE)
    for y in range(Y):
        right = gp[y].reshape(ZL * piece, gp.shape[-1])
        part = lax.dot_general(
            rows[...], right, (((1,), (1,)), ((), ())), preferred_element_type=f32
        ).astype(grad.dtype)
        for x in range(X):
            for zh in range(ZH):
                for c in range(CORE):
                    start = ((x * ZH + zh) * CORE + c) * chunk
                    grad[(x * CORE + c) * Y + y, zh] = part[start : start + chunk]


def fold_kernel(parts, out):
    total = jnp.sum(parts[...].astype(f32), axis=0)
    total = jnp.concatenate([total[z] for z in range(total.shape[0])], axis=0)
    out[...] = total.T.reshape(out.shape)


def fold(parts):
    chunk, lanes = parts.shape[2:]
    return pl.pallas_call(
        fold_kernel,
        out_shape=jax.ShapeDtypeStruct((ZL, lanes // ZL, ZH * chunk), f32),
        in_specs=[vmem()],
        out_specs=vmem(),
        compiler_params=pltpu.CompilerParams(vmem_limit_bytes=VMEM),
        cost_estimate=pl.CostEstimate(flops=32 * 96 * 128, bytes_accessed=1 << 20, transcendentals=0),
        name="fold",
    )(parts)


def dense(rows, w_t, self_part, cotangent):
    hid, nodes = self_part.shape
    width = rows.shape[0]
    chunk, piece = width // (X * ZH * CORE), hid // (ZL * Y)
    return pl.pallas_call(
        dense_kernel,
        out_shape=(
            jax.ShapeDtypeStruct((hid, nodes), bf16),
            jax.ShapeDtypeStruct((X * CORE * Y, ZH, chunk, ZL * piece), bf16),
        ),
        in_specs=[vmem()] * 4,
        out_specs=(vmem(), vmem()),
        scratch_shapes=[pltpu.VMEM((Y, ZL, piece, nodes), bf16)],
        compiler_params=pltpu.CompilerParams(vmem_limit_bytes=VMEM),
        cost_estimate=pl.CostEstimate(flops=4 * 512 * 768 * 128, bytes_accessed=2 << 20, transcendentals=512 * 128),
        name="dense",
    )(rows, w_t, self_part, cotangent)


def onward(value):
    pairs = []
    for z in range(ZH):
        pairs.append((z * CORE, (z + 1) % ZH * CORE))
        pairs.append((z * CORE + 1, (z - 1) % ZH * CORE + 1))
    return lax.ppermute(value, ("zh", "c"), pairs)


def plan(owners, local):
    me = lax.axis_index("zh")
    slots = owners.shape[0]
    core = owners % CORE
    apart = (owners // CORE + ZH - me) % ZH
    server = jnp.where(apart == 3, 0, jnp.where(apart == 1, 1, core))
    second = (apart == 2) | ((apart % 2 == 1) & (server != core))
    held = (apart == 2) | ((apart % 2 == 1) & (server == core))
    column = (owners // (ZH * CORE)) * CORE + server
    group = column + jnp.where(second, X * CORE, 0)
    s = jnp.arange(slots, dtype=jnp.int32)
    earlier = (group[:, None] == group[None, :]) & (s[None, :] < s[:, None])
    rank = jnp.sum(earlier.astype(jnp.int32), axis=1)
    place = column * 2 * EACH + jnp.where(second, EACH, 0) + rank
    hit = place[:, None] == jnp.arange(X * CORE * 2 * EACH, dtype=jnp.int32)[None, :]
    ask = jnp.sum(jnp.where(hit, (held.astype(jnp.int32) * 16 + local)[:, None], 0), axis=0)
    return group * EACH + rank, ask


def exchange(packed):
    return lax.all_to_all(packed, ("x", "c"), 0, 0).reshape((-1,) + packed.shape[2:])


def per_device(features, counts, src_owner, src_local, tiles, w_neigh, self_part, cotangent):
    rows, cols = features.shape
    width = tiles.shape[1]
    node_cols = self_part.shape[1]
    peers = X * CORE
    live = counts[0] > 0

    def asking():
        pos, ask = plan(src_owner[:, 0], src_local)
        other = lax.ppermute(features, "c", [(0, 1), (1, 0)])
        codes = lax.all_to_all(ask.reshape(peers, -1), ("x", "c"), 0, 0)
        return pos, codes.reshape(-1), other

    first = onward(features)
    pos, codes, other = lax.cond(
        live,
        asking,
        lambda: (jnp.zeros_like(src_local), jnp.zeros((2 * peers * EACH,), jnp.int32), jnp.zeros_like(features)),
    )
    codes, first, other = lax.optimization_barrier((codes, first, other))
    late = onward(jnp.concatenate([other[None], first[None]]))
    early = lax.cond(
        live,
        lambda: exchange(pack(codes, (features, first), 0, width)),
        lambda: jnp.zeros((peers * EACH, rows, width), bf16),
    )
    early, late = lax.optimization_barrier((early, late))
    late = exchange(pack(codes, (late,), EACH, width))
    aggregated = aggregate(pos, counts, early, late, tiles, node_cols)
    node_rows = lax.all_to_all(aggregated, ("zl", "y"), 0, 0).reshape(-1, node_cols)
    hidden, grad = dense(node_rows, w_neigh.T, self_part, cotangent)
    grad = fold(lax.all_to_all(grad, ("x", "c", "y"), 0, 0))
    grad = jnp.sum(lax.all_to_all(grad, "zl", 0, 0), axis=0)
    grad = jnp.transpose(grad.reshape(-1, ZH, rows), (1, 0, 2))
    grad_scale = 1.0 / math.sqrt(cols * X * ZH * CORE)
    return hidden, jnp.sum(lax.all_to_all(grad, "zh", 0, 0), axis=0) * grad_scale


def solution(mesh):
    fine = Mesh(mesh.devices.reshape(X, ZH, CORE, ZL, Y), ("x", "zh", "c", "zl", "y"))
    node, feat = ("x", "zh", "c"), ("zl", "y")
    return jax.shard_map(
        per_device,
        mesh=fine,
        in_specs=(
            P(feat, node),
            P(node),
            P(node, None),
            P(node),
            P(node, None, None),
            P(),
            P(None, node + feat),
            P(None, node + feat),
        ),
        out_specs=(P(None, node + feat), P(feat, node)),
        check_vma=False,
    )
```

```python
import math

import jax
import jax.numpy as jnp
from jax import lax
from jax.experimental import pallas as pl
from jax.experimental.pallas import tpu as pltpu
from jax.sharding import Mesh
from jax.sharding import PartitionSpec as P

MAXT = 3
CAP = 4
X, ZH, CORE, ZL, Y = 4, 4, 2, 8, 4
OWN, NEAR, FAR = CAP, 2 * CAP, CAP
PEERS = X * CORE
GROUPS = 4
VMEM = 16 * 1024 * 1024
f32, bf16 = jnp.float32, jnp.bfloat16


def vmem():
    return pl.BlockSpec(memory_space=pltpu.VMEM)


def smem():
    return pl.BlockSpec(memory_space=pltpu.SMEM)


def pack_kernel(first, width, codes, *refs):
    held, out = refs[:-1], refs[-1]
    peers, each = out.shape[0], out.shape[1]
    asked = codes.shape[0] // peers

    def one(d, carry):
        for k in range(each):
            code = codes[d * asked + first + k]
            place = pl.ds(pl.multiple_of(code % 16 * width, width), width)
            block = held[0][:, place]
            if len(held) > 1:
                block = jnp.where(code < 16, block, held[1][:, place])
            out[d, k] = block
        return carry

    lax.fori_loop(0, peers, one, 0, unroll=2)


def pack(codes, held, first, each, width):
    return pl.pallas_call(
        lambda *refs: pack_kernel(first, width, *refs),
        out_shape=jax.ShapeDtypeStruct((PEERS, each, held[0].shape[0], width), held[0].dtype),
        in_specs=[smem()] + [vmem()] * len(held),
        out_specs=vmem(),
        compiler_params=pltpu.CompilerParams(vmem_limit_bytes=VMEM),
        cost_estimate=pl.CostEstimate(flops=0, bytes_accessed=2 << 20, transcendentals=0),
        name="pack",
    )(codes, *held)


def agg_kernel(pos, counts, own, near, far, tiles_in, out, tiles, arrived):
    second, third = own.shape[0], own.shape[0] + near.shape[0]
    half = out.shape[-1]
    per = tiles.shape[1] // half
    groups = arrived.shape[0]
    size = counts.shape[0] // groups

    def fetch(g):
        part = pl.ds(g * size * MAXT, size * MAXT)
        return pltpu.make_async_copy(tiles_in.at[part], tiles.at[part], arrived.at[g])

    for g in range(groups):
        fetch(g).start()

    def one(g, carry):
        fetch(g).wait()
        for b in [g * size + i for i in range(size)]:
            count = counts[b]
            total = None
            for m in range(MAXT):
                p = pos[b * MAXT + m]
                block = jnp.where(
                    p < second,
                    own[jnp.minimum(p, second - 1)],
                    jnp.where(
                        p < third,
                        near[jnp.clip(p - second, 0, near.shape[0] - 1)],
                        far[jnp.maximum(p - third, 0)],
                    ),
                )
                block = jnp.where(m < count, block, jnp.zeros_like(block))
                part = lax.dot_general(
                    block, tiles[b * MAXT + m], (((1,), (1,)), ((), ())), preferred_element_type=f32
                )
                total = part if m == 0 else total + part
            total = (total / count.astype(f32)).astype(out.dtype)
            for j in range(per):
                out[b * per + j] = total[:, j * half : (j + 1) * half]
        return carry

    lax.fori_loop(0, groups, one, 0)


def aggregate(pos, counts, own, near, far, tiles, node_cols):
    rows, width = own.shape[1:]
    return pl.pallas_call(
        agg_kernel,
        out_shape=jax.ShapeDtypeStruct((counts.shape[0] * width // node_cols, rows, node_cols), bf16),
        in_specs=[smem(), smem(), vmem(), vmem(), vmem(), pl.BlockSpec(memory_space=pltpu.HBM)],
        out_specs=vmem(),
        scratch_shapes=[pltpu.VMEM(tiles.shape, tiles.dtype), pltpu.SemaphoreType.DMA((GROUPS,))],
        compiler_params=pltpu.CompilerParams(vmem_limit_bytes=50 * 1024 * 1024),
        cost_estimate=pl.CostEstimate(flops=2 * 48 * 24 * 65536, bytes_accessed=7 << 20, transcendentals=0),
        name="aggregate",
    )(pos, counts, own, near, far, tiles)


def dense_kernel(rows, w_t, self_part, cotangent, hidden, grad, gp):
    pre = jnp.dot(w_t[...], rows[...], preferred_element_type=f32) + self_part[...].astype(f32)
    sig = jax.nn.sigmoid(pre)
    hidden[...] = (pre * sig).astype(hidden.dtype)
    slope = sig * (1.0 + pre * (1.0 - sig))
    grad_pre = (cotangent[...].astype(f32) * slope).astype(bf16)
    piece = grad_pre.shape[0] // (ZL * Y)
    for zl in range(ZL):
        for y in range(Y):
            start = (zl * Y + y) * piece
            gp[y, zl] = grad_pre[start : start + piece]
    chunk = rows.shape[0] // (X * ZH * CORE)
    for y in range(Y):
        right = gp[y].reshape(ZL * piece, gp.shape[-1])
        part = lax.dot_general(
            rows[...], right, (((1,), (1,)), ((), ())), preferred_element_type=f32
        ).astype(grad.dtype)
        for x in range(X):
            for zh in range(ZH):
                for c in range(CORE):
                    start = ((x * ZH + zh) * CORE + c) * chunk
                    grad[(x * CORE + c) * Y + y, zh] = part[start : start + chunk]


def fold_kernel(parts, out):
    total = jnp.sum(parts[...].astype(f32), axis=0)
    total = jnp.concatenate([total[z] for z in range(total.shape[0])], axis=0)
    out[...] = total.T.reshape(out.shape)


def fold(parts):
    chunk, lanes = parts.shape[2:]
    return pl.pallas_call(
        fold_kernel,
        out_shape=jax.ShapeDtypeStruct((ZL, lanes // ZL, ZH * chunk), f32),
        in_specs=[vmem()],
        out_specs=vmem(),
        compiler_params=pltpu.CompilerParams(vmem_limit_bytes=VMEM),
        cost_estimate=pl.CostEstimate(flops=32 * 96 * 128, bytes_accessed=1 << 20, transcendentals=0),
        name="fold",
    )(parts)


def dense(rows, w_t, self_part, cotangent):
    hid, nodes = self_part.shape
    width = rows.shape[0]
    chunk, piece = width // (X * ZH * CORE), hid // (ZL * Y)
    return pl.pallas_call(
        dense_kernel,
        out_shape=(
            jax.ShapeDtypeStruct((hid, nodes), bf16),
            jax.ShapeDtypeStruct((X * CORE * Y, ZH, chunk, ZL * piece), bf16),
        ),
        in_specs=[vmem()] * 4,
        out_specs=(vmem(), vmem()),
        scratch_shapes=[pltpu.VMEM((Y, ZL, piece, nodes), bf16)],
        compiler_params=pltpu.CompilerParams(vmem_limit_bytes=VMEM),
        cost_estimate=pl.CostEstimate(flops=4 * 512 * 768 * 128, bytes_accessed=2 << 20, transcendentals=512 * 128),
        name="dense",
    )(rows, w_t, self_part, cotangent)


def onward(value):
    pairs = []
    for z in range(ZH):
        pairs.append((z * CORE, (z + 1) % ZH * CORE))
        pairs.append((z * CORE + 1, (z - 1) % ZH * CORE + 1))
    return lax.ppermute(value, ("zh", "c"), pairs)


def plan(owners, local):
    me = lax.axis_index("zh")
    slots = owners.shape[0]
    core = owners % CORE
    apart = (owners // CORE + ZH - me) % ZH
    server = jnp.where(apart == 3, 0, jnp.where(apart == 1, 1, core))
    column = (owners // (ZH * CORE)) * CORE + server
    near, far = apart % 2 == 1, apart == 2
    group = column + jnp.where(far, 2 * PEERS, jnp.where(near, PEERS, 0))
    s = jnp.arange(slots, dtype=jnp.int32)
    earlier = (group[:, None] == group[None, :]) & (s[None, :] < s[:, None])
    rank = jnp.sum(earlier.astype(jnp.int32), axis=1)
    pos = rank + jnp.where(
        far,
        PEERS * (OWN + NEAR) + column * FAR,
        jnp.where(near, PEERS * OWN + column * NEAR, column * OWN),
    )
    place = column * (OWN + NEAR + FAR) + rank + jnp.where(far, OWN + NEAR, jnp.where(near, OWN, 0))
    code = local + jnp.where(near & (server != core), 16, 0)
    hit = place[:, None] == jnp.arange(PEERS * (OWN + NEAR + FAR), dtype=jnp.int32)[None, :]
    return pos, jnp.sum(jnp.where(hit, code[:, None], 0), axis=0)


def exchange(packed):
    return lax.all_to_all(packed, ("x", "c"), 0, 0).reshape((-1,) + packed.shape[2:])


def per_device(features, counts, src_owner, src_local, tiles, w_neigh, self_part, cotangent):
    rows, cols = features.shape
    width = tiles.shape[1]
    node_cols = self_part.shape[1]
    live = counts[0] > 0

    def beside(work, *like):
        return lax.cond(live, work, lambda: tuple(jnp.zeros(shape, kind) for shape, kind in like))

    def asking():
        pos, ask = plan(src_owner[:, 0], src_local)
        other = lax.ppermute(features, "c", [(0, 1), (1, 0)])
        codes = lax.all_to_all(ask.reshape(PEERS, -1), ("x", "c"), 0, 0)
        return pos, codes.reshape(-1), other

    first = onward(features)
    pos, codes, other = beside(
        asking,
        (src_local.shape, jnp.int32),
        ((PEERS * (OWN + NEAR + FAR),), jnp.int32),
        (features.shape, bf16),
    )
    second = onward(other)
    (own,) = beside(
        lambda: (exchange(pack(codes, (features,), 0, OWN, width)),), ((PEERS * OWN, rows, width), bf16)
    )
    own, first = lax.optimization_barrier((own, first))
    third = onward(first)
    (near,) = beside(
        lambda: (exchange(pack(codes, (first, second), OWN, NEAR, width)),), ((PEERS * NEAR, rows, width), bf16)
    )
    near, third = lax.optimization_barrier((near, third))
    far = exchange(pack(codes, (third,), OWN + NEAR, FAR, width))
    aggregated = aggregate(pos, counts, own, near, far, tiles, node_cols)
    node_rows = lax.all_to_all(aggregated, ("zl", "y"), 0, 0).reshape(-1, node_cols)
    hidden, grad = dense(node_rows, w_neigh.T, self_part, cotangent)
    grad = fold(lax.all_to_all(grad, ("x", "c", "y"), 0, 0))
    grad = jnp.sum(lax.all_to_all(grad, "zl", 0, 0), axis=0)
    grad = jnp.transpose(grad.reshape(-1, ZH, rows), (1, 0, 2))
    grad_scale = 1.0 / math.sqrt(cols * X * ZH * CORE)
    return hidden, jnp.sum(lax.all_to_all(grad, "zh", 0, 0), axis=0) * grad_scale


def solution(mesh):
    fine = Mesh(mesh.devices.reshape(X, ZH, CORE, ZL, Y), ("x", "zh", "c", "zl", "y"))
    node, feat = ("x", "zh", "c"), ("zl", "y")
    return jax.shard_map(
        per_device,
        mesh=fine,
        in_specs=(
            P(feat, node),
            P(node),
            P(node, None),
            P(node),
            P(node, None, None),
            P(),
            P(None, node + feat),
            P(None, node + feat),
        ),
        out_specs=(P(None, node + feat), P(feat, node)),
        check_vma=False,
    )
```

```python
import math

import jax
import jax.numpy as jnp
from jax import lax
from jax.experimental import pallas as pl
from jax.experimental.pallas import tpu as pltpu
from jax.sharding import Mesh
from jax.sharding import PartitionSpec as P

MAXT = 3
CAP = 4
X, ZH, CORE, ZL, Y = 4, 4, 2, 8, 4
NEAR, FAR = 3 * CAP, CAP
PEERS = X * CORE
GROUPS = 4
VMEM = 16 * 1024 * 1024
f32, bf16 = jnp.float32, jnp.bfloat16


def vmem():
    return pl.BlockSpec(memory_space=pltpu.VMEM)


def smem():
    return pl.BlockSpec(memory_space=pltpu.SMEM)


def pack_kernel(first, width, codes, *refs):
    held, out = refs[:-1], refs[-1]
    peers, each = out.shape[0], out.shape[1]
    asked = codes.shape[0] // peers

    def one(d, carry):
        for k in range(each):
            code = codes[d * asked + first + k]
            place = pl.ds(pl.multiple_of(code % 16 * width, width), width)
            block = held[0][:, place]
            for j in range(1, len(held)):
                block = jnp.where(code < 16 * j, block, held[j][:, place])
            out[d, k] = block
        return carry

    lax.fori_loop(0, peers, one, 0, unroll=2)


def pack(codes, held, first, each, width):
    return pl.pallas_call(
        lambda *refs: pack_kernel(first, width, *refs),
        out_shape=jax.ShapeDtypeStruct((PEERS, each, held[0].shape[0], width), held[0].dtype),
        in_specs=[smem()] + [vmem()] * len(held),
        out_specs=vmem(),
        compiler_params=pltpu.CompilerParams(vmem_limit_bytes=VMEM),
        cost_estimate=pl.CostEstimate(flops=0, bytes_accessed=2 << 20, transcendentals=0),
        name="pack",
    )(codes, *held)


def agg_kernel(pos, counts, near, far, tiles_in, out, tiles, arrived):
    size_near = near.shape[0]
    half = out.shape[-1]
    per = tiles.shape[1] // half
    groups = arrived.shape[0]
    size = counts.shape[0] // groups

    def fetch(g):
        part = pl.ds(g * size * MAXT, size * MAXT)
        return pltpu.make_async_copy(tiles_in.at[part], tiles.at[part], arrived.at[g])

    for g in range(groups):
        fetch(g).start()

    def one(g, carry):
        fetch(g).wait()
        for b in [g * size + i for i in range(size)]:
            count = counts[b]
            total = None
            for m in range(MAXT):
                p = pos[b * MAXT + m]
                block = jnp.where(
                    p < size_near,
                    near[jnp.minimum(p, size_near - 1)],
                    far[jnp.maximum(p - size_near, 0)],
                )
                block = jnp.where(m < count, block, jnp.zeros_like(block))
                part = lax.dot_general(
                    block, tiles[b * MAXT + m], (((1,), (1,)), ((), ())), preferred_element_type=f32
                )
                total = part if m == 0 else total + part
            total = (total / count.astype(f32)).astype(out.dtype)
            for j in range(per):
                out[b * per + j] = total[:, j * half : (j + 1) * half]
        return carry

    lax.fori_loop(0, groups, one, 0)


def aggregate(pos, counts, near, far, tiles, node_cols):
    rows, width = near.shape[1:]
    return pl.pallas_call(
        agg_kernel,
        out_shape=jax.ShapeDtypeStruct((counts.shape[0] * width // node_cols, rows, node_cols), bf16),
        in_specs=[smem(), smem(), vmem(), vmem(), pl.BlockSpec(memory_space=pltpu.HBM)],
        out_specs=vmem(),
        scratch_shapes=[pltpu.VMEM(tiles.shape, tiles.dtype), pltpu.SemaphoreType.DMA((GROUPS,))],
        compiler_params=pltpu.CompilerParams(vmem_limit_bytes=50 * 1024 * 1024),
        cost_estimate=pl.CostEstimate(flops=2 * 48 * 24 * 65536, bytes_accessed=7 << 20, transcendentals=0),
        name="aggregate",
    )(pos, counts, near, far, tiles)


def dense_kernel(rows, w_t, self_part, cotangent, hidden, grad, gp):
    pre = jnp.dot(w_t[...], rows[...], preferred_element_type=f32) + self_part[...].astype(f32)
    sig = jax.nn.sigmoid(pre)
    hidden[...] = (pre * sig).astype(hidden.dtype)
    slope = sig * (1.0 + pre * (1.0 - sig))
    grad_pre = (cotangent[...].astype(f32) * slope).astype(bf16)
    piece = grad_pre.shape[0] // (ZL * Y)
    for zl in range(ZL):
        for y in range(Y):
            start = (zl * Y + y) * piece
            gp[y, zl] = grad_pre[start : start + piece]
    chunk = rows.shape[0] // (X * ZH * CORE)
    for y in range(Y):
        right = gp[y].reshape(ZL * piece, gp.shape[-1])
        part = lax.dot_general(
            rows[...], right, (((1,), (1,)), ((), ())), preferred_element_type=f32
        ).astype(grad.dtype)
        for x in range(X):
            for zh in range(ZH):
                for c in range(CORE):
                    start = ((x * ZH + zh) * CORE + c) * chunk
                    grad[(x * CORE + c) * Y + y, zh] = part[start : start + chunk]


def fold_kernel(parts, out):
    total = jnp.sum(parts[...].astype(f32), axis=0)
    total = jnp.concatenate([total[z] for z in range(total.shape[0])], axis=0)
    out[...] = total.T.reshape(out.shape)


def fold(parts):
    chunk, lanes = parts.shape[2:]
    return pl.pallas_call(
        fold_kernel,
        out_shape=jax.ShapeDtypeStruct((ZL, lanes // ZL, ZH * chunk), f32),
        in_specs=[vmem()],
        out_specs=vmem(),
        compiler_params=pltpu.CompilerParams(vmem_limit_bytes=VMEM),
        cost_estimate=pl.CostEstimate(flops=32 * 96 * 128, bytes_accessed=1 << 20, transcendentals=0),
        name="fold",
    )(parts)


def dense(rows, w_t, self_part, cotangent):
    hid, nodes = self_part.shape
    width = rows.shape[0]
    chunk, piece = width // (X * ZH * CORE), hid // (ZL * Y)
    return pl.pallas_call(
        dense_kernel,
        out_shape=(
            jax.ShapeDtypeStruct((hid, nodes), bf16),
            jax.ShapeDtypeStruct((X * CORE * Y, ZH, chunk, ZL * piece), bf16),
        ),
        in_specs=[vmem()] * 4,
        out_specs=(vmem(), vmem()),
        scratch_shapes=[pltpu.VMEM((Y, ZL, piece, nodes), bf16)],
        compiler_params=pltpu.CompilerParams(vmem_limit_bytes=VMEM),
        cost_estimate=pl.CostEstimate(flops=4 * 512 * 768 * 128, bytes_accessed=2 << 20, transcendentals=512 * 128),
        name="dense",
    )(rows, w_t, self_part, cotangent)


def onward(value):
    pairs = []
    for z in range(ZH):
        pairs.append((z * CORE, (z + 1) % ZH * CORE))
        pairs.append((z * CORE + 1, (z - 1) % ZH * CORE + 1))
    return lax.ppermute(value, ("zh", "c"), pairs)


def plan(owners, local):
    me = lax.axis_index("zh")
    slots = owners.shape[0]
    core = owners % CORE
    apart = (owners // CORE + ZH - me) % ZH
    server = jnp.where(apart == 3, 0, jnp.where(apart == 1, 1, core))
    column = (owners // (ZH * CORE)) * CORE + server
    far = apart == 2
    group = column + jnp.where(far, PEERS, 0)
    s = jnp.arange(slots, dtype=jnp.int32)
    earlier = (group[:, None] == group[None, :]) & (s[None, :] < s[:, None])
    rank = jnp.sum(earlier.astype(jnp.int32), axis=1)
    pos = rank + jnp.where(far, PEERS * NEAR + column * FAR, column * NEAR)
    place = column * (NEAR + FAR) + rank + jnp.where(far, NEAR, 0)
    code = local + jnp.where(apart % 2 == 1, jnp.where(server == core, 16, 32), 0)
    hit = place[:, None] == jnp.arange(PEERS * (NEAR + FAR), dtype=jnp.int32)[None, :]
    return pos, jnp.sum(jnp.where(hit, code[:, None], 0), axis=0)


def exchange(packed):
    return lax.all_to_all(packed, ("x", "c"), 0, 0).reshape((-1,) + packed.shape[2:])


def per_device(features, counts, src_owner, src_local, tiles, w_neigh, self_part, cotangent):
    rows, cols = features.shape
    width = tiles.shape[1]
    node_cols = self_part.shape[1]
    live = counts[0] > 0

    def beside(work, *like):
        return lax.cond(live, work, lambda: tuple(jnp.zeros(shape, kind) for shape, kind in like))

    def asking():
        pos, ask = plan(src_owner[:, 0], src_local)
        other = lax.ppermute(features, "c", [(0, 1), (1, 0)])
        codes = lax.all_to_all(ask.reshape(PEERS, -1), ("x", "c"), 0, 0)
        return pos, codes.reshape(-1), other

    first = onward(features)
    pos, codes, other = beside(
        asking,
        (src_local.shape, jnp.int32),
        ((PEERS * (NEAR + FAR),), jnp.int32),
        (features.shape, bf16),
    )
    second = onward(other)
    third = onward(first)
    (near,) = beside(
        lambda: (exchange(pack(codes, (features, first, second), 0, NEAR, width)),),
        ((PEERS * NEAR, rows, width), bf16),
    )
    near, third = lax.optimization_barrier((near, third))
    far = exchange(pack(codes, (third,), NEAR, FAR, width))
    aggregated = aggregate(pos, counts, near, far, tiles, node_cols)
    node_rows = lax.all_to_all(aggregated, ("zl", "y"), 0, 0).reshape(-1, node_cols)
    hidden, grad = dense(node_rows, w_neigh.T, self_part, cotangent)
    grad = fold(lax.all_to_all(grad, ("x", "c", "y"), 0, 0))
    grad = jnp.sum(lax.all_to_all(grad, "zl", 0, 0), axis=0)
    grad = jnp.transpose(grad.reshape(-1, ZH, rows), (1, 0, 2))
    grad_scale = 1.0 / math.sqrt(cols * X * ZH * CORE)
    return hidden, jnp.sum(lax.all_to_all(grad, "zh", 0, 0), axis=0) * grad_scale


def solution(mesh):
    fine = Mesh(mesh.devices.reshape(X, ZH, CORE, ZL, Y), ("x", "zh", "c", "zl", "y"))
    node, feat = ("x", "zh", "c"), ("zl", "y")
    return jax.shard_map(
        per_device,
        mesh=fine,
        in_specs=(
            P(feat, node),
            P(node),
            P(node, None),
            P(node),
            P(node, None, None),
            P(),
            P(None, node + feat),
            P(None, node + feat),
        ),
        out_specs=(P(None, node + feat), P(feat, node)),
        check_vma=False,
    )
```

```python
import math

import jax
import jax.numpy as jnp
from jax import lax
from jax.experimental import pallas as pl
from jax.experimental.pallas import tpu as pltpu
from jax.sharding import Mesh
from jax.sharding import PartitionSpec as P

MAXT = 3
CAP = 4
X, ZH, CORE, ZL, Y = 4, 4, 2, 8, 4
OWN, NEAR, FAR = CAP, 2 * CAP, CAP
PEERS = X * CORE
LANES = 128
GROUPS = 4
VMEM = 16 * 1024 * 1024
f32, bf16 = jnp.float32, jnp.bfloat16


def vmem():
    return pl.BlockSpec(memory_space=pltpu.VMEM)


def smem():
    return pl.BlockSpec(memory_space=pltpu.SMEM)


def pack_kernel(first, width, codes, *refs):
    held, out = refs[:-1], refs[-1]
    peers, each = out.shape[0], out.shape[1]
    asked = codes.shape[0] // peers

    def one(d, carry):
        for k in range(each):
            code = codes[d * asked + first + k]
            place = pl.ds(pl.multiple_of(code % 16 * width, width), width)
            block = held[0][:, place]
            if len(held) > 1:
                block = jnp.where(code < 16, block, held[1][:, place])
            out[d, k] = block
        return carry

    lax.fori_loop(0, peers, one, 0, unroll=2)


def pack(codes, held, first, each, width):
    return pl.pallas_call(
        lambda *refs: pack_kernel(first, width, *refs),
        out_shape=jax.ShapeDtypeStruct((PEERS, each, held[0].shape[0], width), held[0].dtype),
        in_specs=[smem()] + [vmem()] * len(held),
        out_specs=vmem(),
        compiler_params=pltpu.CompilerParams(vmem_limit_bytes=VMEM),
        cost_estimate=pl.CostEstimate(flops=0, bytes_accessed=2 << 20, transcendentals=0),
        name="pack",
    )(codes, *held)


def agg_kernel(pos, counts, own, near, far, tiles_in, out, tiles, arrived):
    second, third = own.shape[0], own.shape[0] + near.shape[0]
    half = out.shape[-1]
    per = tiles.shape[1] // half
    groups = arrived.shape[0]
    size = counts.shape[0] // groups

    def fetch(g):
        part = pl.ds(g * size * MAXT, size * MAXT)
        return pltpu.make_async_copy(tiles_in.at[part], tiles.at[part], arrived.at[g])

    for g in range(groups):
        fetch(g).start()

    def one(g, carry):
        fetch(g).wait()
        for b in [g * size + i for i in range(size)]:
            count = counts[b]
            total = None
            for m in range(MAXT):
                p = pos[b * MAXT + m]
                block = jnp.where(
                    p < second,
                    own[jnp.minimum(p, second - 1)],
                    jnp.where(
                        p < third,
                        near[jnp.clip(p - second, 0, near.shape[0] - 1)],
                        far[jnp.maximum(p - third, 0)],
                    ),
                )
                block = jnp.where(m < count, block, jnp.zeros_like(block))
                part = lax.dot_general(
                    block, tiles[b * MAXT + m], (((1,), (1,)), ((), ())), preferred_element_type=f32
                )
                total = part if m == 0 else total + part
            total = (total / count.astype(f32)).astype(out.dtype)
            for j in range(per):
                out[b * per + j] = total[:, j * half : (j + 1) * half]
        return carry

    lax.fori_loop(0, groups, one, 0)


def aggregate(pos, counts, own, near, far, tiles, node_cols):
    rows, width = own.shape[1:]
    return pl.pallas_call(
        agg_kernel,
        out_shape=jax.ShapeDtypeStruct((counts.shape[0] * width // node_cols, rows, node_cols), bf16),
        in_specs=[smem(), smem(), vmem(), vmem(), vmem(), pl.BlockSpec(memory_space=pltpu.HBM)],
        out_specs=vmem(),
        scratch_shapes=[pltpu.VMEM(tiles.shape, tiles.dtype), pltpu.SemaphoreType.DMA((GROUPS,))],
        compiler_params=pltpu.CompilerParams(vmem_limit_bytes=50 * 1024 * 1024),
        cost_estimate=pl.CostEstimate(flops=2 * 48 * 24 * 65536, bytes_accessed=7 << 20, transcendentals=0),
        name="aggregate",
    )(pos, counts, own, near, far, tiles)


def dense_kernel(rows, w_t, self_part, cotangent, hidden, grad, gp):
    pre = jnp.dot(w_t[...], rows[...], preferred_element_type=f32) + self_part[...].astype(f32)
    sig = jax.nn.sigmoid(pre)
    hidden[...] = (pre * sig).astype(hidden.dtype)
    slope = sig * (1.0 + pre * (1.0 - sig))
    grad_pre = (cotangent[...].astype(f32) * slope).astype(bf16)
    piece = grad_pre.shape[0] // (ZL * Y)
    for zl in range(ZL):
        for y in range(Y):
            start = (zl * Y + y) * piece
            gp[y, zl] = grad_pre[start : start + piece]
    chunk = rows.shape[0] // (X * ZH * CORE)
    for y in range(Y):
        right = gp[y].reshape(ZL * piece, gp.shape[-1])
        part = lax.dot_general(
            rows[...], right, (((1,), (1,)), ((), ())), preferred_element_type=f32
        ).astype(grad.dtype)
        for x in range(X):
            for zh in range(ZH):
                for c in range(CORE):
                    start = ((x * ZH + zh) * CORE + c) * chunk
                    grad[(x * CORE + c) * Y + y, zh] = part[start : start + chunk]


def fold_kernel(parts, out):
    total = jnp.sum(parts[...].astype(f32), axis=0)
    total = jnp.concatenate([total[z] for z in range(total.shape[0])], axis=0)
    out[...] = total.T.reshape(out.shape)


def fold(parts):
    chunk, lanes = parts.shape[2:]
    return pl.pallas_call(
        fold_kernel,
        out_shape=jax.ShapeDtypeStruct((ZL, lanes // ZL, ZH * chunk), f32),
        in_specs=[vmem()],
        out_specs=vmem(),
        compiler_params=pltpu.CompilerParams(vmem_limit_bytes=VMEM),
        cost_estimate=pl.CostEstimate(flops=32 * 96 * 128, bytes_accessed=1 << 20, transcendentals=0),
        name="fold",
    )(parts)


def dense(rows, w_t, self_part, cotangent):
    hid, nodes = self_part.shape
    width = rows.shape[0]
    chunk, piece = width // (X * ZH * CORE), hid // (ZL * Y)
    return pl.pallas_call(
        dense_kernel,
        out_shape=(
            jax.ShapeDtypeStruct((hid, nodes), bf16),
            jax.ShapeDtypeStruct((X * CORE * Y, ZH, chunk, ZL * piece), bf16),
        ),
        in_specs=[vmem()] * 4,
        out_specs=(vmem(), vmem()),
        scratch_shapes=[pltpu.VMEM((Y, ZL, piece, nodes), bf16)],
        compiler_params=pltpu.CompilerParams(vmem_limit_bytes=VMEM),
        cost_estimate=pl.CostEstimate(flops=4 * 512 * 768 * 128, bytes_accessed=2 << 20, transcendentals=512 * 128),
        name="dense",
    )(rows, w_t, self_part, cotangent)


def onward(value, step):
    pairs = []
    for z in range(ZH):
        pairs.append((z * CORE, (z + step) % ZH * CORE))
        pairs.append((z * CORE + 1, (z - step) % ZH * CORE + 1))
    return lax.ppermute(value, ("zh", "c"), pairs)


def plan(owners, local):
    me = lax.axis_index("zh")
    slots = owners.shape[0]
    core = owners % CORE
    column = (owners // (ZH * CORE)) * CORE + core
    apart = (me + ZH - owners // CORE % ZH) % ZH
    apart = jnp.where(core == 0, apart, (ZH - apart) % ZH)
    near, far = apart % 2 == 1, apart == 2
    group = column + jnp.where(far, 2 * PEERS, jnp.where(near, PEERS, 0))
    s = jnp.arange(slots, dtype=jnp.int32)
    earlier = (group[:, None] == group[None, :]) & (s[None, :] < s[:, None])
    rank = jnp.sum(earlier.astype(jnp.int32), axis=1)
    pos = rank + jnp.where(
        far,
        PEERS * (OWN + NEAR) + column * FAR,
        jnp.where(near, PEERS * OWN + column * NEAR, column * OWN),
    )
    place = column * LANES + rank + jnp.where(far, OWN + NEAR, jnp.where(near, OWN, 0))
    code = local + jnp.where(apart == 3, 16, 0)
    hit = place[:, None] == jnp.arange(PEERS * LANES, dtype=jnp.int32)[None, :]
    return pos, jnp.sum(jnp.where(hit, code[:, None], 0), axis=0)


def exchange(packed):
    return lax.all_to_all(packed, ("x", "c"), 0, 0).reshape((-1,) + packed.shape[2:])


def per_device(features, counts, src_owner, src_local, tiles, w_neigh, self_part, cotangent):
    rows, cols = features.shape
    width = tiles.shape[1]
    node_cols = self_part.shape[1]
    live = counts[0] > 0

    def beside(work, *like):
        return lax.cond(live, work, lambda: tuple(jnp.zeros(shape, kind) for shape, kind in like))

    def asking():
        pos, ask = plan(src_owner[:, 0], src_local)
        codes = lax.all_to_all(ask.reshape(PEERS, 1, LANES), ("x", "c"), 0, 0)
        return pos, codes.reshape(-1)

    first = onward(features, 1)
    pos, codes = beside(
        asking,
        (src_local.shape, jnp.int32),
        ((PEERS * LANES,), jnp.int32),
    )
    codes, again = lax.optimization_barrier((codes, features))
    second = onward(again, -1)
    (own,) = beside(
        lambda: (exchange(pack(codes, (features,), 0, OWN, width)),), ((PEERS * OWN, rows, width), bf16)
    )
    own, first = lax.optimization_barrier((own, first))
    third = onward(first, 1)
    (near,) = beside(
        lambda: (exchange(pack(codes, (first, second), OWN, NEAR, width)),), ((PEERS * NEAR, rows, width), bf16)
    )
    near, third = lax.optimization_barrier((near, third))
    far = exchange(pack(codes, (third,), OWN + NEAR, FAR, width))
    aggregated = aggregate(pos, counts, own, near, far, tiles, node_cols)
    node_rows = lax.all_to_all(aggregated, ("zl", "y"), 0, 0).reshape(-1, node_cols)
    hidden, grad = dense(node_rows, w_neigh.T, self_part, cotangent)
    grad = fold(lax.all_to_all(grad, ("x", "c", "y"), 0, 0))
    grad = jnp.sum(lax.all_to_all(grad, "zl", 0, 0), axis=0)
    grad = jnp.transpose(grad.reshape(-1, ZH, rows), (1, 0, 2))
    grad = lax.all_to_all(jnp.pad(grad, ((0, 0), (0, 0), (0, LANES - rows))), "zh", 0, 0)
    grad_scale = 1.0 / math.sqrt(cols * X * ZH * CORE)
    return hidden, jnp.sum(grad, axis=0)[:, :rows] * grad_scale


def solution(mesh):
    fine = Mesh(mesh.devices.reshape(X, ZH, CORE, ZL, Y), ("x", "zh", "c", "zl", "y"))
    node, feat = ("x", "zh", "c"), ("zl", "y")
    return jax.shard_map(
        per_device,
        mesh=fine,
        in_specs=(
            P(feat, node),
            P(node),
            P(node, None),
            P(node),
            P(node, None, None),
            P(),
            P(None, node + feat),
            P(None, node + feat),
        ),
        out_specs=(P(None, node + feat), P(feat, node)),
        check_vma=False,
    )
```

```python
import math

import jax
import jax.numpy as jnp
from jax import lax
from jax.experimental import pallas as pl
from jax.experimental.pallas import tpu as pltpu
from jax.sharding import Mesh
from jax.sharding import PartitionSpec as P

MAXT = 3
CAP = 4
X, ZH, CORE, ZL, Y = 4, 4, 2, 8, 4
OWN, NEAR, FAR = CAP, 2 * CAP, CAP
PEERS = X * CORE
LANES = 128
GROUPS = 4
VMEM = 16 * 1024 * 1024
f32, bf16 = jnp.float32, jnp.bfloat16


def vmem():
    return pl.BlockSpec(memory_space=pltpu.VMEM)


def smem():
    return pl.BlockSpec(memory_space=pltpu.SMEM)


def pack_kernel(first, width, codes, *refs):
    held, out = refs[:-1], refs[-1]
    peers, each = out.shape[0], out.shape[1]
    asked = codes.shape[0] // peers

    def one(d, carry):
        for k in range(each):
            code = codes[d * asked + first + k]
            place = pl.ds(pl.multiple_of(code % 16 * width, width), width)
            block = held[0][:, place]
            if len(held) > 1:
                block = jnp.where(code < 16, block, held[1][:, place])
            out[d, k] = block
        return carry

    lax.fori_loop(0, peers, one, 0, unroll=2)


def pack(codes, held, first, each, width):
    return pl.pallas_call(
        lambda *refs: pack_kernel(first, width, *refs),
        out_shape=jax.ShapeDtypeStruct((PEERS, each, held[0].shape[0], width), held[0].dtype),
        in_specs=[smem()] + [vmem()] * len(held),
        out_specs=vmem(),
        compiler_params=pltpu.CompilerParams(vmem_limit_bytes=VMEM),
        cost_estimate=pl.CostEstimate(flops=0, bytes_accessed=2 << 20, transcendentals=0),
        name="pack",
    )(codes, *held)


def agg_kernel(pos, counts, own, near, far, tiles_in, out, tiles, arrived):
    second, third = own.shape[0], own.shape[0] + near.shape[0]
    half = out.shape[-1]
    per = tiles.shape[1] // half
    groups = arrived.shape[0]
    size = counts.shape[0] // groups

    def fetch(g):
        part = pl.ds(g * size * MAXT, size * MAXT)
        return pltpu.make_async_copy(tiles_in.at[part], tiles.at[part], arrived.at[g])

    for g in range(groups):
        fetch(g).start()

    def one(g, carry):
        fetch(g).wait()
        for b in [g * size + i for i in range(size)]:
            count = counts[b]
            total = None
            for m in range(MAXT):
                p = pos[b * MAXT + m]
                block = jnp.where(
                    p < second,
                    own[jnp.minimum(p, second - 1)],
                    jnp.where(
                        p < third,
                        near[jnp.clip(p - second, 0, near.shape[0] - 1)],
                        far[jnp.maximum(p - third, 0)],
                    ),
                )
                block = jnp.where(m < count, block, jnp.zeros_like(block))
                part = lax.dot_general(
                    block, tiles[b * MAXT + m], (((1,), (1,)), ((), ())), preferred_element_type=f32
                )
                total = part if m == 0 else total + part
            total = (total / count.astype(f32)).astype(out.dtype)
            for j in range(per):
                out[b * per + j] = total[:, j * half : (j + 1) * half]
        return carry

    lax.fori_loop(0, groups, one, 0)


def aggregate(pos, counts, own, near, far, tiles, node_cols):
    rows, width = own.shape[1:]
    return pl.pallas_call(
        agg_kernel,
        out_shape=jax.ShapeDtypeStruct((counts.shape[0] * width // node_cols, rows, node_cols), bf16),
        in_specs=[smem(), smem(), vmem(), vmem(), vmem(), pl.BlockSpec(memory_space=pltpu.HBM)],
        out_specs=vmem(),
        scratch_shapes=[pltpu.VMEM(tiles.shape, tiles.dtype), pltpu.SemaphoreType.DMA((GROUPS,))],
        compiler_params=pltpu.CompilerParams(vmem_limit_bytes=50 * 1024 * 1024),
        cost_estimate=pl.CostEstimate(flops=2 * 48 * 24 * 65536, bytes_accessed=7 << 20, transcendentals=0),
        name="aggregate",
    )(pos, counts, own, near, far, tiles)


def dense_kernel(rows, w_t, self_part, cotangent, hidden, grad, gp):
    pre = jnp.dot(w_t[...], rows[...], preferred_element_type=f32) + self_part[...].astype(f32)
    sig = jax.nn.sigmoid(pre)
    hidden[...] = (pre * sig).astype(hidden.dtype)
    slope = sig * (1.0 + pre * (1.0 - sig))
    grad_pre = (cotangent[...].astype(f32) * slope).astype(bf16)
    piece = grad_pre.shape[0] // (ZL * Y)
    for zl in range(ZL):
        for y in range(Y):
            start = (zl * Y + y) * piece
            gp[y, zl] = grad_pre[start : start + piece]
    chunk = rows.shape[0] // (X * ZH * CORE)
    for y in range(Y):
        right = gp[y].reshape(ZL * piece, gp.shape[-1])
        part = lax.dot_general(
            rows[...], right, (((1,), (1,)), ((), ())), preferred_element_type=f32
        ).astype(grad.dtype)
        for x in range(X):
            for zh in range(ZH):
                for c in range(CORE):
                    start = ((x * ZH + zh) * CORE + c) * chunk
                    grad[(x * CORE + c) * Y + y, zh] = part[start : start + chunk]


def fold_kernel(parts, out):
    total = jnp.sum(parts[...].astype(f32), axis=0)
    total = jnp.concatenate([total[z] for z in range(total.shape[0])], axis=0)
    out[...] = total.T.reshape(out.shape)


def fold(parts):
    chunk, lanes = parts.shape[2:]
    return pl.pallas_call(
        fold_kernel,
        out_shape=jax.ShapeDtypeStruct((ZL, lanes // ZL, ZH * chunk), f32),
        in_specs=[vmem()],
        out_specs=vmem(),
        compiler_params=pltpu.CompilerParams(vmem_limit_bytes=VMEM),
        cost_estimate=pl.CostEstimate(flops=32 * 96 * 128, bytes_accessed=1 << 20, transcendentals=0),
        name="fold",
    )(parts)


def dense(rows, w_t, self_part, cotangent):
    hid, nodes = self_part.shape
    width = rows.shape[0]
    chunk, piece = width // (X * ZH * CORE), hid // (ZL * Y)
    return pl.pallas_call(
        dense_kernel,
        out_shape=(
            jax.ShapeDtypeStruct((hid, nodes), bf16),
            jax.ShapeDtypeStruct((X * CORE * Y, ZH, chunk, ZL * piece), bf16),
        ),
        in_specs=[vmem()] * 4,
        out_specs=(vmem(), vmem()),
        scratch_shapes=[pltpu.VMEM((Y, ZL, piece, nodes), bf16)],
        compiler_params=pltpu.CompilerParams(vmem_limit_bytes=VMEM),
        cost_estimate=pl.CostEstimate(flops=4 * 512 * 768 * 128, bytes_accessed=2 << 20, transcendentals=512 * 128),
        name="dense",
    )(rows, w_t, self_part, cotangent)


def onward(value, step):
    pairs = []
    for z in range(ZH):
        pairs.append((z * CORE, (z + step) % ZH * CORE))
        pairs.append((z * CORE + 1, (z - step) % ZH * CORE + 1))
    return lax.ppermute(value, ("zh", "c"), pairs)


def plan(owners, local):
    me = lax.axis_index("zh")
    slots = owners.shape[0]
    core = owners % CORE
    column = (owners // (ZH * CORE)) * CORE + core
    apart = (me + ZH - owners // CORE % ZH) % ZH
    apart = jnp.where(core == 0, apart, (ZH - apart) % ZH)
    near, far = apart % 2 == 1, apart == 2
    group = column + jnp.where(far, 2 * PEERS, jnp.where(near, PEERS, 0))
    s = jnp.arange(slots, dtype=jnp.int32)
    earlier = (group[:, None] == group[None, :]) & (s[None, :] < s[:, None])
    rank = jnp.sum(earlier.astype(jnp.int32), axis=1)
    pos = rank + jnp.where(
        far,
        PEERS * (OWN + NEAR) + column * FAR,
        jnp.where(near, PEERS * OWN + column * NEAR, column * OWN),
    )
    place = column * LANES + rank + jnp.where(far, OWN + NEAR, jnp.where(near, OWN, 0))
    code = local + jnp.where(apart == 3, 16, 0)
    hit = place[:, None] == jnp.arange(PEERS * LANES, dtype=jnp.int32)[None, :]
    return pos, jnp.sum(jnp.where(hit, code[:, None], 0), axis=0)


def exchange(packed):
    return lax.all_to_all(packed, ("x", "c"), 0, 0).reshape((-1,) + packed.shape[2:])


def per_device(features, counts, src_owner, src_local, tiles, w_neigh, self_part, cotangent):
    rows, cols = features.shape
    width = tiles.shape[1]
    node_cols = self_part.shape[1]
    live = counts[0] > 0

    def beside(work, *like):
        return lax.cond(live, work, lambda: tuple(jnp.zeros(shape, kind) for shape, kind in like))

    def asking():
        pos, ask = plan(src_owner[:, 0], src_local)
        codes = lax.all_to_all(ask.reshape(PEERS, 1, LANES), ("x", "c"), 0, 0).reshape(-1)
        return pos, codes, exchange(pack(codes, (features,), 0, OWN, width))

    first = onward(features, 1)
    second = onward(features, -1)
    pos, codes, own = beside(
        asking,
        (src_local.shape, jnp.int32),
        ((PEERS * LANES,), jnp.int32),
        ((PEERS * OWN, rows, width), bf16),
    )
    own, first = lax.optimization_barrier((own, first))
    third = onward(first, 1)
    (near,) = beside(
        lambda: (exchange(pack(codes, (first, second), OWN, NEAR, width)),), ((PEERS * NEAR, rows, width), bf16)
    )
    near, third = lax.optimization_barrier((near, third))
    far = exchange(pack(codes, (third,), OWN + NEAR, FAR, width))
    aggregated = aggregate(pos, counts, own, near, far, tiles, node_cols)
    node_rows = lax.all_to_all(aggregated, ("zl", "y"), 0, 0).reshape(-1, node_cols)
    hidden, grad = dense(node_rows, w_neigh.T, self_part, cotangent)
    grad = fold(lax.all_to_all(grad, ("x", "c", "y"), 0, 0))
    grad = jnp.sum(lax.all_to_all(grad, "zl", 0, 0), axis=0)
    grad = jnp.transpose(grad.reshape(-1, ZH, rows), (1, 0, 2))
    grad = lax.all_to_all(jnp.pad(grad, ((0, 0), (0, 0), (0, LANES - rows))), "zh", 0, 0)
    grad_scale = 1.0 / math.sqrt(cols * X * ZH * CORE)
    return hidden, jnp.sum(grad, axis=0)[:, :rows] * grad_scale


def solution(mesh):
    fine = Mesh(mesh.devices.reshape(X, ZH, CORE, ZL, Y), ("x", "zh", "c", "zl", "y"))
    node, feat = ("x", "zh", "c"), ("zl", "y")
    return jax.shard_map(
        per_device,
        mesh=fine,
        in_specs=(
            P(feat, node),
            P(node),
            P(node, None),
            P(node),
            P(node, None, None),
            P(),
            P(None, node + feat),
            P(None, node + feat),
        ),
        out_specs=(P(None, node + feat), P(feat, node)),
        check_vma=False,
    )
```

```python
import math

import jax
import jax.numpy as jnp
from jax import lax
from jax.experimental import pallas as pl
from jax.experimental.pallas import tpu as pltpu
from jax.sharding import Mesh
from jax.sharding import PartitionSpec as P

MAXT = 3
CAP = 4
X, ZH, CORE, ZL, Y = 4, 4, 2, 8, 4
NEAR, FAR = 3 * CAP, CAP
PEERS = X * CORE
LANES = 128
GROUPS = 4
VMEM = 16 * 1024 * 1024
f32, bf16 = jnp.float32, jnp.bfloat16


def vmem():
    return pl.BlockSpec(memory_space=pltpu.VMEM)


def smem():
    return pl.BlockSpec(memory_space=pltpu.SMEM)


def pack_kernel(first, width, codes, *refs):
    held, out = refs[:-1], refs[-1]
    peers, each = out.shape[0], out.shape[1]
    asked = codes.shape[0] // peers

    def one(d, carry):
        for k in range(each):
            code = codes[d * asked + first + k]
            place = pl.ds(pl.multiple_of(code % 16 * width, width), width)
            block = held[0][:, place]
            for j in range(1, len(held)):
                block = jnp.where(code < 16 * j, block, held[j][:, place])
            out[d, k] = block
        return carry

    lax.fori_loop(0, peers, one, 0, unroll=2)


def pack(codes, held, first, each, width):
    return pl.pallas_call(
        lambda *refs: pack_kernel(first, width, *refs),
        out_shape=jax.ShapeDtypeStruct((PEERS, each, held[0].shape[0], width), held[0].dtype),
        in_specs=[smem()] + [vmem()] * len(held),
        out_specs=vmem(),
        compiler_params=pltpu.CompilerParams(vmem_limit_bytes=VMEM),
        cost_estimate=pl.CostEstimate(flops=0, bytes_accessed=2 << 20, transcendentals=0),
        name="pack",
    )(codes, *held)


def agg_kernel(pos, counts, near, far, tiles_in, out, tiles, arrived):
    size_near = near.shape[0]
    half = out.shape[-1]
    per = tiles.shape[1] // half
    groups = arrived.shape[0]
    size = counts.shape[0] // groups

    def fetch(g):
        part = pl.ds(g * size * MAXT, size * MAXT)
        return pltpu.make_async_copy(tiles_in.at[part], tiles.at[part], arrived.at[g])

    for g in range(groups):
        fetch(g).start()

    def one(g, carry):
        fetch(g).wait()
        for b in [g * size + i for i in range(size)]:
            count = counts[b]
            total = None
            for m in range(MAXT):
                p = pos[b * MAXT + m]
                block = jnp.where(
                    p < size_near,
                    near[jnp.minimum(p, size_near - 1)],
                    far[jnp.maximum(p - size_near, 0)],
                )
                block = jnp.where(m < count, block, jnp.zeros_like(block))
                part = lax.dot_general(
                    block, tiles[b * MAXT + m], (((1,), (1,)), ((), ())), preferred_element_type=f32
                )
                total = part if m == 0 else total + part
            total = (total / count.astype(f32)).astype(out.dtype)
            for j in range(per):
                out[b * per + j] = total[:, j * half : (j + 1) * half]
        return carry

    lax.fori_loop(0, groups, one, 0)


def aggregate(pos, counts, near, far, tiles, node_cols):
    rows, width = near.shape[1:]
    return pl.pallas_call(
        agg_kernel,
        out_shape=jax.ShapeDtypeStruct((counts.shape[0] * width // node_cols, rows, node_cols), bf16),
        in_specs=[smem(), smem(), vmem(), vmem(), pl.BlockSpec(memory_space=pltpu.HBM)],
        out_specs=vmem(),
        scratch_shapes=[pltpu.VMEM(tiles.shape, tiles.dtype), pltpu.SemaphoreType.DMA((GROUPS,))],
        compiler_params=pltpu.CompilerParams(vmem_limit_bytes=50 * 1024 * 1024),
        cost_estimate=pl.CostEstimate(flops=2 * 48 * 24 * 65536, bytes_accessed=7 << 20, transcendentals=0),
        name="aggregate",
    )(pos, counts, near, far, tiles)


def dense_kernel(rows, w_t, self_part, cotangent, hidden, grad, gp):
    pre = jnp.dot(w_t[...], rows[...], preferred_element_type=f32) + self_part[...].astype(f32)
    sig = jax.nn.sigmoid(pre)
    hidden[...] = (pre * sig).astype(hidden.dtype)
    slope = sig * (1.0 + pre * (1.0 - sig))
    grad_pre = (cotangent[...].astype(f32) * slope).astype(bf16)
    piece = grad_pre.shape[0] // (ZL * Y)
    for zl in range(ZL):
        for y in range(Y):
            start = (zl * Y + y) * piece
            gp[y, zl] = grad_pre[start : start + piece]
    chunk = rows.shape[0] // (X * ZH * CORE)
    for y in range(Y):
        right = gp[y].reshape(ZL * piece, gp.shape[-1])
        part = lax.dot_general(
            rows[...], right, (((1,), (1,)), ((), ())), preferred_element_type=f32
        ).astype(grad.dtype)
        for x in range(X):
            for zh in range(ZH):
                for c in range(CORE):
                    start = ((x * ZH + zh) * CORE + c) * chunk
                    grad[(x * CORE + c) * Y + y, zh] = part[start : start + chunk]


def fold_kernel(parts, out):
    total = jnp.sum(parts[...].astype(f32), axis=0)
    total = jnp.concatenate([total[z] for z in range(total.shape[0])], axis=0)
    out[...] = total.T.reshape(out.shape)


def fold(parts):
    chunk, lanes = parts.shape[2:]
    return pl.pallas_call(
        fold_kernel,
        out_shape=jax.ShapeDtypeStruct((ZL, lanes // ZL, ZH * chunk), f32),
        in_specs=[vmem()],
        out_specs=vmem(),
        compiler_params=pltpu.CompilerParams(vmem_limit_bytes=VMEM),
        cost_estimate=pl.CostEstimate(flops=32 * 96 * 128, bytes_accessed=1 << 20, transcendentals=0),
        name="fold",
    )(parts)


def dense(rows, w_t, self_part, cotangent):
    hid, nodes = self_part.shape
    width = rows.shape[0]
    chunk, piece = width // (X * ZH * CORE), hid // (ZL * Y)
    return pl.pallas_call(
        dense_kernel,
        out_shape=(
            jax.ShapeDtypeStruct((hid, nodes), bf16),
            jax.ShapeDtypeStruct((X * CORE * Y, ZH, chunk, ZL * piece), bf16),
        ),
        in_specs=[vmem()] * 4,
        out_specs=(vmem(), vmem()),
        scratch_shapes=[pltpu.VMEM((Y, ZL, piece, nodes), bf16)],
        compiler_params=pltpu.CompilerParams(vmem_limit_bytes=VMEM),
        cost_estimate=pl.CostEstimate(flops=4 * 512 * 768 * 128, bytes_accessed=2 << 20, transcendentals=512 * 128),
        name="dense",
    )(rows, w_t, self_part, cotangent)


def onward(value, step):
    pairs = []
    for z in range(ZH):
        pairs.append((z * CORE, (z + step) % ZH * CORE))
        pairs.append((z * CORE + 1, (z - step) % ZH * CORE + 1))
    return lax.ppermute(value, ("zh", "c"), pairs)


def plan(owners, local):
    me = lax.axis_index("zh")
    slots = owners.shape[0]
    core = owners % CORE
    column = (owners // (ZH * CORE)) * CORE + core
    apart = (me + ZH - owners // CORE % ZH) % ZH
    apart = jnp.where(core == 0, apart, (ZH - apart) % ZH)
    far = apart == 2
    group = column + jnp.where(far, PEERS, 0)
    s = jnp.arange(slots, dtype=jnp.int32)
    earlier = (group[:, None] == group[None, :]) & (s[None, :] < s[:, None])
    rank = jnp.sum(earlier.astype(jnp.int32), axis=1)
    pos = rank + jnp.where(far, PEERS * NEAR + column * FAR, column * NEAR)
    place = column * LANES + rank + jnp.where(far, NEAR, 0)
    code = local + jnp.where(apart == 1, 16, jnp.where(apart == 3, 32, 0))
    hit = place[:, None] == jnp.arange(PEERS * LANES, dtype=jnp.int32)[None, :]
    return pos, jnp.sum(jnp.where(hit, code[:, None], 0), axis=0)


def exchange(packed):
    return lax.all_to_all(packed, ("x", "c"), 0, 0).reshape((-1,) + packed.shape[2:])


def per_device(features, counts, src_owner, src_local, tiles, w_neigh, self_part, cotangent):
    rows, cols = features.shape
    width = tiles.shape[1]
    node_cols = self_part.shape[1]
    live = counts[0] > 0

    def beside(work, *like):
        return lax.cond(live, work, lambda: tuple(jnp.zeros(shape, kind) for shape, kind in like))

    def asking():
        pos, ask = plan(src_owner[:, 0], src_local)
        return pos, lax.all_to_all(ask.reshape(PEERS, 1, LANES), ("x", "c"), 0, 0).reshape(-1)

    first = onward(features, 1)
    second = onward(features, -1)
    pos, codes = beside(asking, (src_local.shape, jnp.int32), ((PEERS * LANES,), jnp.int32))
    codes, first = lax.optimization_barrier((codes, first))
    third = onward(first, 1)
    (near,) = beside(
        lambda: (exchange(pack(codes, (features, first, second), 0, NEAR, width)),),
        ((PEERS * NEAR, rows, width), bf16),
    )
    near, third = lax.optimization_barrier((near, third))
    far = exchange(pack(codes, (third,), NEAR, FAR, width))
    aggregated = aggregate(pos, counts, near, far, tiles, node_cols)
    node_rows = lax.all_to_all(aggregated, ("zl", "y"), 0, 0).reshape(-1, node_cols)
    hidden, grad = dense(node_rows, w_neigh.T, self_part, cotangent)
    grad = fold(lax.all_to_all(grad, ("x", "c", "y"), 0, 0))
    grad = jnp.sum(lax.all_to_all(grad, "zl", 0, 0), axis=0)
    grad = jnp.transpose(grad.reshape(-1, ZH, rows), (1, 0, 2))
    grad = lax.all_to_all(jnp.pad(grad, ((0, 0), (0, 0), (0, LANES - rows))), "zh", 0, 0)
    grad_scale = 1.0 / math.sqrt(cols * X * ZH * CORE)
    return hidden, jnp.sum(grad, axis=0)[:, :rows] * grad_scale


def solution(mesh):
    fine = Mesh(mesh.devices.reshape(X, ZH, CORE, ZL, Y), ("x", "zh", "c", "zl", "y"))
    node, feat = ("x", "zh", "c"), ("zl", "y")
    return jax.shard_map(
        per_device,
        mesh=fine,
        in_specs=(
            P(feat, node),
            P(node),
            P(node, None),
            P(node),
            P(node, None, None),
            P(),
            P(None, node + feat),
            P(None, node + feat),
        ),
        out_specs=(P(None, node + feat), P(feat, node)),
        check_vma=False,
    )
```

```python
import math

import jax
import jax.numpy as jnp
from jax import lax
from jax.experimental import pallas as pl
from jax.experimental.pallas import tpu as pltpu
from jax.sharding import Mesh
from jax.sharding import PartitionSpec as P

MAXT = 3
CAP = 4
X, ZH, CORE, ZL, Y = 4, 4, 2, 8, 4
NEAR, FAR = 2 * CAP, 2 * CAP
PEERS = X * CORE
LANES = 128
GROUPS = 4
VMEM = 16 * 1024 * 1024
f32, bf16 = jnp.float32, jnp.bfloat16


def vmem():
    return pl.BlockSpec(memory_space=pltpu.VMEM)


def smem():
    return pl.BlockSpec(memory_space=pltpu.SMEM)


def pack_kernel(first, width, codes, *refs):
    held, out = refs[:-1], refs[-1]
    peers, each = out.shape[0], out.shape[1]
    asked = codes.shape[0] // peers

    def one(d, carry):
        for k in range(each):
            code = codes[d * asked + first + k]
            place = pl.ds(pl.multiple_of(code % 16 * width, width), width)
            block = held[0][:, place]
            for j in range(1, len(held)):
                block = jnp.where(code < 16 * j, block, held[j][:, place])
            out[d, k] = block
        return carry

    lax.fori_loop(0, peers, one, 0, unroll=2)


def pack(codes, held, first, each, width):
    return pl.pallas_call(
        lambda *refs: pack_kernel(first, width, *refs),
        out_shape=jax.ShapeDtypeStruct((PEERS, each, held[0].shape[0], width), held[0].dtype),
        in_specs=[smem()] + [vmem()] * len(held),
        out_specs=vmem(),
        compiler_params=pltpu.CompilerParams(vmem_limit_bytes=VMEM),
        cost_estimate=pl.CostEstimate(flops=0, bytes_accessed=2 << 20, transcendentals=0),
        name="pack",
    )(codes, *held)


def agg_kernel(pos, counts, near, far, tiles_in, out, tiles, arrived):
    size_near = near.shape[0]
    half = out.shape[-1]
    per = tiles.shape[1] // half
    groups = arrived.shape[0]
    size = counts.shape[0] // groups

    def fetch(g):
        part = pl.ds(g * size * MAXT, size * MAXT)
        return pltpu.make_async_copy(tiles_in.at[part], tiles.at[part], arrived.at[g])

    for g in range(groups):
        fetch(g).start()

    def one(g, carry):
        fetch(g).wait()
        for b in [g * size + i for i in range(size)]:
            count = counts[b]
            total = None
            for m in range(MAXT):
                p = pos[b * MAXT + m]
                block = jnp.where(
                    p < size_near,
                    near[jnp.minimum(p, size_near - 1)],
                    far[jnp.maximum(p - size_near, 0)],
                )
                block = jnp.where(m < count, block, jnp.zeros_like(block))
                part = lax.dot_general(
                    block, tiles[b * MAXT + m], (((1,), (1,)), ((), ())), preferred_element_type=f32
                )
                total = part if m == 0 else total + part
            total = (total / count.astype(f32)).astype(out.dtype)
            for j in range(per):
                out[b * per + j] = total[:, j * half : (j + 1) * half]
        return carry

    lax.fori_loop(0, groups, one, 0)


def aggregate(pos, counts, near, far, tiles, node_cols):
    rows, width = near.shape[1:]
    return pl.pallas_call(
        agg_kernel,
        out_shape=jax.ShapeDtypeStruct((counts.shape[0] * width // node_cols, rows, node_cols), bf16),
        in_specs=[smem(), smem(), vmem(), vmem(), pl.BlockSpec(memory_space=pltpu.HBM)],
        out_specs=vmem(),
        scratch_shapes=[pltpu.VMEM(tiles.shape, tiles.dtype), pltpu.SemaphoreType.DMA((GROUPS,))],
        compiler_params=pltpu.CompilerParams(vmem_limit_bytes=50 * 1024 * 1024),
        cost_estimate=pl.CostEstimate(flops=2 * 48 * 24 * 65536, bytes_accessed=7 << 20, transcendentals=0),
        name="aggregate",
    )(pos, counts, near, far, tiles)


def dense_kernel(rows, w_t, self_part, cotangent, hidden, grad, gp):
    pre = jnp.dot(w_t[...], rows[...], preferred_element_type=f32) + self_part[...].astype(f32)
    sig = jax.nn.sigmoid(pre)
    hidden[...] = (pre * sig).astype(hidden.dtype)
    slope = sig * (1.0 + pre * (1.0 - sig))
    grad_pre = (cotangent[...].astype(f32) * slope).astype(bf16)
    piece = grad_pre.shape[0] // (ZL * Y)
    for zl in range(ZL):
        for y in range(Y):
            start = (zl * Y + y) * piece
            gp[y, zl] = grad_pre[start : start + piece]
    chunk = rows.shape[0] // (X * ZH * CORE)
    for y in range(Y):
        right = gp[y].reshape(ZL * piece, gp.shape[-1])
        part = lax.dot_general(
            rows[...], right, (((1,), (1,)), ((), ())), preferred_element_type=f32
        ).astype(grad.dtype)
        for x in range(X):
            for zh in range(ZH):
                for c in range(CORE):
                    start = ((x * ZH + zh) * CORE + c) * chunk
                    grad[(x * CORE + c) * Y + y, zh] = part[start : start + chunk]


def fold_kernel(parts, out):
    total = jnp.sum(parts[...].astype(f32), axis=0)
    total = jnp.concatenate([total[z] for z in range(total.shape[0])], axis=0)
    out[...] = total.T.reshape(out.shape)


def fold(parts):
    chunk, lanes = parts.shape[2:]
    return pl.pallas_call(
        fold_kernel,
        out_shape=jax.ShapeDtypeStruct((ZL, lanes // ZL, ZH * chunk), f32),
        in_specs=[vmem()],
        out_specs=vmem(),
        compiler_params=pltpu.CompilerParams(vmem_limit_bytes=VMEM),
        cost_estimate=pl.CostEstimate(flops=32 * 96 * 128, bytes_accessed=1 << 20, transcendentals=0),
        name="fold",
    )(parts)


def dense(rows, w_t, self_part, cotangent):
    hid, nodes = self_part.shape
    width = rows.shape[0]
    chunk, piece = width // (X * ZH * CORE), hid // (ZL * Y)
    return pl.pallas_call(
        dense_kernel,
        out_shape=(
            jax.ShapeDtypeStruct((hid, nodes), bf16),
            jax.ShapeDtypeStruct((X * CORE * Y, ZH, chunk, ZL * piece), bf16),
        ),
        in_specs=[vmem()] * 4,
        out_specs=(vmem(), vmem()),
        scratch_shapes=[pltpu.VMEM((Y, ZL, piece, nodes), bf16)],
        compiler_params=pltpu.CompilerParams(vmem_limit_bytes=VMEM),
        cost_estimate=pl.CostEstimate(flops=4 * 512 * 768 * 128, bytes_accessed=2 << 20, transcendentals=512 * 128),
        name="dense",
    )(rows, w_t, self_part, cotangent)


def onward(value, step):
    pairs = []
    for z in range(ZH):
        pairs.append((z * CORE, (z + step) % ZH * CORE))
        pairs.append((z * CORE + 1, (z - step) % ZH * CORE + 1))
    return lax.ppermute(value, ("zh", "c"), pairs)


def plan(owners, local):
    me = lax.axis_index("zh")
    slots = owners.shape[0]
    core = owners % CORE
    column = (owners // (ZH * CORE)) * CORE + core
    apart = (me + ZH - owners // CORE % ZH) % ZH
    apart = jnp.where(core == 0, apart, (ZH - apart) % ZH)
    far = apart > 1
    group = column + jnp.where(far, PEERS, 0)
    s = jnp.arange(slots, dtype=jnp.int32)
    earlier = (group[:, None] == group[None, :]) & (s[None, :] < s[:, None])
    rank = jnp.sum(earlier.astype(jnp.int32), axis=1)
    pos = rank + jnp.where(far, PEERS * NEAR + column * FAR, column * NEAR)
    place = column * LANES + rank + jnp.where(far, NEAR, 0)
    code = local + jnp.where((apart == 1) | (apart == 2), 16, 0)
    hit = place[:, None] == jnp.arange(PEERS * LANES, dtype=jnp.int32)[None, :]
    return pos, jnp.sum(jnp.where(hit, code[:, None], 0), axis=0)


def exchange(packed):
    return lax.all_to_all(packed, ("x", "c"), 0, 0).reshape((-1,) + packed.shape[2:])


def per_device(features, counts, src_owner, src_local, tiles, w_neigh, self_part, cotangent):
    rows, cols = features.shape
    width = tiles.shape[1]
    node_cols = self_part.shape[1]
    live = counts[0] > 0

    def beside(work, *like):
        return lax.cond(live, work, lambda: tuple(jnp.zeros(shape, kind) for shape, kind in like))

    def asking():
        pos, ask = plan(src_owner[:, 0], src_local)
        return pos, lax.all_to_all(ask.reshape(PEERS, 1, LANES), ("x", "c"), 0, 0).reshape(-1)

    first = onward(features, 1)
    pos, codes = beside(asking, (src_local.shape, jnp.int32), ((PEERS * LANES,), jnp.int32))
    codes, again = lax.optimization_barrier((codes, features))
    second = onward(again, -1)
    codes, first = lax.optimization_barrier((codes, first))
    third = onward(first, 1)
    (near,) = beside(
        lambda: (exchange(pack(codes, (features, first), 0, NEAR, width)),),
        ((PEERS * NEAR, rows, width), bf16),
    )
    near, second, third = lax.optimization_barrier((near, second, third))
    far = exchange(pack(codes, (second, third), NEAR, FAR, width))
    aggregated = aggregate(pos, counts, near, far, tiles, node_cols)
    node_rows = lax.all_to_all(aggregated, ("zl", "y"), 0, 0).reshape(-1, node_cols)
    hidden, grad = dense(node_rows, w_neigh.T, self_part, cotangent)
    grad = fold(lax.all_to_all(grad, ("x", "c", "y"), 0, 0))
    grad = jnp.sum(lax.all_to_all(grad, "zl", 0, 0), axis=0)
    grad = jnp.transpose(grad.reshape(-1, ZH, rows), (1, 0, 2))
    grad = lax.all_to_all(jnp.pad(grad, ((0, 0), (0, 0), (0, LANES - rows))), "zh", 0, 0)
    grad_scale = 1.0 / math.sqrt(cols * X * ZH * CORE)
    return hidden, jnp.sum(grad, axis=0)[:, :rows] * grad_scale


def solution(mesh):
    fine = Mesh(mesh.devices.reshape(X, ZH, CORE, ZL, Y), ("x", "zh", "c", "zl", "y"))
    node, feat = ("x", "zh", "c"), ("zl", "y")
    return jax.shard_map(
        per_device,
        mesh=fine,
        in_specs=(
            P(feat, node),
            P(node),
            P(node, None),
            P(node),
            P(node, None, None),
            P(),
            P(None, node + feat),
            P(None, node + feat),
        ),
        out_specs=(P(None, node + feat), P(feat, node)),
        check_vma=False,
    )
```

```python
import math

import jax
import jax.numpy as jnp
from jax import lax
from jax.experimental import pallas as pl
from jax.experimental.pallas import tpu as pltpu
from jax.sharding import Mesh
from jax.sharding import PartitionSpec as P

MAXT = 3
CAP = 4
X, ZH, CORE, ZL, Y = 4, 4, 2, 8, 4
OWN, NEAR, FAR = CAP, 2 * CAP, CAP
PEERS = X * CORE
LANES = 128
GROUPS = 4
VMEM = 16 * 1024 * 1024
f32, bf16 = jnp.float32, jnp.bfloat16


def vmem():
    return pl.BlockSpec(memory_space=pltpu.VMEM)


def smem():
    return pl.BlockSpec(memory_space=pltpu.SMEM)


def pack_kernel(first, width, codes, *refs):
    held, out = refs[:-1], refs[-1]
    peers, each = out.shape[0], out.shape[1]
    asked = codes.shape[0] // peers

    def one(d, carry):
        for k in range(each):
            code = codes[d * asked + first + k]
            place = pl.ds(pl.multiple_of(code % 16 * width, width), width)
            block = held[0][:, place]
            if len(held) > 1:
                block = jnp.where(code < 16, block, held[1][:, place])
            out[d, k] = block
        return carry

    lax.fori_loop(0, peers, one, 0, unroll=2)


def pack(codes, held, first, each, width):
    return pl.pallas_call(
        lambda *refs: pack_kernel(first, width, *refs),
        out_shape=jax.ShapeDtypeStruct((PEERS, each, held[0].shape[0], width), held[0].dtype),
        in_specs=[smem()] + [vmem()] * len(held),
        out_specs=vmem(),
        compiler_params=pltpu.CompilerParams(vmem_limit_bytes=VMEM),
        cost_estimate=pl.CostEstimate(flops=0, bytes_accessed=2 << 20, transcendentals=0),
        name="pack",
    )(codes, *held)


def agg_kernel(pos, counts, own, near, far, tiles_in, out, tiles, arrived):
    second, third = own.shape[0], own.shape[0] + near.shape[0]
    half = out.shape[-1]
    per = tiles.shape[1] // half
    groups = arrived.shape[0]
    size = counts.shape[0] // groups

    def fetch(g):
        part = pl.ds(g * size * MAXT, size * MAXT)
        return pltpu.make_async_copy(tiles_in.at[part], tiles.at[part], arrived.at[g])

    for g in range(groups):
        fetch(g).start()

    def one(g, carry):
        fetch(g).wait()
        for b in [g * size + i for i in range(size)]:
            count = counts[b]
            total = None
            for m in range(MAXT):
                p = pos[b * MAXT + m]
                block = jnp.where(
                    p < second,
                    own[jnp.minimum(p, second - 1)],
                    jnp.where(
                        p < third,
                        near[jnp.clip(p - second, 0, near.shape[0] - 1)],
                        far[jnp.maximum(p - third, 0)],
                    ),
                )
                block = jnp.where(m < count, block, jnp.zeros_like(block))
                part = lax.dot_general(
                    block, tiles[b * MAXT + m], (((1,), (1,)), ((), ())), preferred_element_type=f32
                )
                total = part if m == 0 else total + part
            total = (total / count.astype(f32)).astype(out.dtype)
            for j in range(per):
                out[b * per + j] = total[:, j * half : (j + 1) * half]
        return carry

    lax.fori_loop(0, groups, one, 0)


def aggregate(pos, counts, own, near, far, tiles, node_cols):
    rows, width = own.shape[1:]
    return pl.pallas_call(
        agg_kernel,
        out_shape=jax.ShapeDtypeStruct((counts.shape[0] * width // node_cols, rows, node_cols), bf16),
        in_specs=[smem(), smem(), vmem(), vmem(), vmem(), pl.BlockSpec(memory_space=pltpu.HBM)],
        out_specs=vmem(),
        scratch_shapes=[pltpu.VMEM(tiles.shape, tiles.dtype), pltpu.SemaphoreType.DMA((GROUPS,))],
        compiler_params=pltpu.CompilerParams(vmem_limit_bytes=50 * 1024 * 1024),
        cost_estimate=pl.CostEstimate(flops=2 * 48 * 24 * 65536, bytes_accessed=7 << 20, transcendentals=0),
        name="aggregate",
    )(pos, counts, own, near, far, tiles)


def dense_kernel(rows, w_t, self_part, cotangent, hidden, grad, gp):
    pre = jnp.dot(w_t[...], rows[...], preferred_element_type=f32) + self_part[...].astype(f32)
    sig = jax.nn.sigmoid(pre)
    hidden[...] = (pre * sig).astype(hidden.dtype)
    slope = sig * (1.0 + pre * (1.0 - sig))
    grad_pre = (cotangent[...].astype(f32) * slope).astype(bf16)
    piece = grad_pre.shape[0] // (ZL * Y)
    for zl in range(ZL):
        for y in range(Y):
            start = (zl * Y + y) * piece
            gp[y, zl] = grad_pre[start : start + piece]
    chunk = rows.shape[0] // (X * ZH * CORE)
    for y in range(Y):
        right = gp[y].reshape(ZL * piece, gp.shape[-1])
        part = lax.dot_general(
            rows[...], right, (((1,), (1,)), ((), ())), preferred_element_type=f32
        ).astype(grad.dtype)
        for x in range(X):
            for zh in range(ZH):
                for c in range(CORE):
                    start = ((x * ZH + zh) * CORE + c) * chunk
                    grad[(x * CORE + c) * Y + y, zh] = part[start : start + chunk]


def fold_kernel(parts, out):
    total = jnp.sum(parts[...].astype(f32), axis=0)
    total = jnp.concatenate([total[z] for z in range(total.shape[0])], axis=0)
    out[...] = total.T.reshape(out.shape)


def fold(parts):
    chunk, lanes = parts.shape[2:]
    return pl.pallas_call(
        fold_kernel,
        out_shape=jax.ShapeDtypeStruct((ZL, lanes // ZL, ZH * chunk), f32),
        in_specs=[vmem()],
        out_specs=vmem(),
        compiler_params=pltpu.CompilerParams(vmem_limit_bytes=VMEM),
        cost_estimate=pl.CostEstimate(flops=32 * 96 * 128, bytes_accessed=1 << 20, transcendentals=0),
        name="fold",
    )(parts)


def dense(rows, w_t, self_part, cotangent):
    hid, nodes = self_part.shape
    width = rows.shape[0]
    chunk, piece = width // (X * ZH * CORE), hid // (ZL * Y)
    return pl.pallas_call(
        dense_kernel,
        out_shape=(
            jax.ShapeDtypeStruct((hid, nodes), bf16),
            jax.ShapeDtypeStruct((X * CORE * Y, ZH, chunk, ZL * piece), bf16),
        ),
        in_specs=[vmem()] * 4,
        out_specs=(vmem(), vmem()),
        scratch_shapes=[pltpu.VMEM((Y, ZL, piece, nodes), bf16)],
        compiler_params=pltpu.CompilerParams(vmem_limit_bytes=VMEM),
        cost_estimate=pl.CostEstimate(flops=4 * 512 * 768 * 128, bytes_accessed=2 << 20, transcendentals=512 * 128),
        name="dense",
    )(rows, w_t, self_part, cotangent)


def onward(value, step):
    pairs = []
    for z in range(ZH):
        pairs.append((z * CORE, (z + step) % ZH * CORE))
        pairs.append((z * CORE + 1, (z - step) % ZH * CORE + 1))
    return lax.ppermute(value, ("zh", "c"), pairs)


def plan_kernel(here, owner_in, local_in, pos, ask):
    slots = owner_in.shape[0]
    s = lax.broadcasted_iota(jnp.int32, (slots, slots), 0)
    t = lax.broadcasted_iota(jnp.int32, (slots, slots), 1)

    def row(column):
        return jnp.sum(jnp.where(s == t, column, 0.0), axis=0, keepdims=True)

    owners = owner_in[...]
    local = jnp.sum(jnp.where(s == t, local_in[...].astype(f32), 0.0), axis=1, keepdims=True).astype(jnp.int32)
    core = owners & (CORE - 1)
    column = (owners >> 3) * CORE + core
    apart = (here[0] + ZH - ((owners >> 1) & (ZH - 1))) & (ZH - 1)
    apart = jnp.where(core == 0, apart, (ZH - apart) & (ZH - 1))
    near, far = (apart & 1) == 1, apart == 2
    group = column + jnp.where(far, 2 * PEERS, jnp.where(near, PEERS, 0))
    earlier = (group.astype(f32) == row(group.astype(f32))) & (t < s)
    rank = jnp.sum(jnp.where(earlier, 1.0, 0.0), axis=1, keepdims=True).astype(jnp.int32)
    there = rank + jnp.where(
        far,
        PEERS * (OWN + NEAR) + column * FAR,
        jnp.where(near, PEERS * OWN + column * NEAR, column * OWN),
    )
    pos[...] = row(there.astype(f32)).astype(jnp.int32)
    place = rank + jnp.where(far, OWN + NEAR, jnp.where(near, OWN, 0))
    code = (local + jnp.where(apart == 3, 16, 0)).astype(f32)
    lane = lax.broadcasted_iota(jnp.int32, (slots, LANES), 1)
    for d in range(PEERS):
        hit = (lane == place) & (column == d)
        ask[d] = jnp.sum(jnp.where(hit, code, 0.0), axis=0, keepdims=True).astype(jnp.int32)


def plan(owners, local):
    slots = local.shape[0]
    pos, ask = pl.pallas_call(
        plan_kernel,
        out_shape=(
            jax.ShapeDtypeStruct((1, slots), jnp.int32),
            jax.ShapeDtypeStruct((PEERS, 1, LANES), jnp.int32),
        ),
        in_specs=[smem(), vmem(), vmem()],
        out_specs=(vmem(), vmem()),
        compiler_params=pltpu.CompilerParams(vmem_limit_bytes=VMEM),
        name="plan",
    )(lax.axis_index("zh").reshape(1), owners, local.reshape(1, slots))
    return pos.reshape(slots), ask


def exchange(packed):
    return lax.all_to_all(packed, ("x", "c"), 0, 0).reshape((-1,) + packed.shape[2:])


def per_device(features, counts, src_owner, src_local, tiles, w_neigh, self_part, cotangent):
    rows, cols = features.shape
    width = tiles.shape[1]
    node_cols = self_part.shape[1]
    live = counts[0] > 0

    def beside(work, *like):
        return lax.cond(live, work, lambda: tuple(jnp.zeros(shape, kind) for shape, kind in like))

    def asking():
        pos, ask = plan(src_owner, src_local)
        codes = lax.all_to_all(ask, ("x", "c"), 0, 0)
        return pos, codes.reshape(-1)

    first = onward(features, 1)
    pos, codes = beside(
        asking,
        (src_local.shape, jnp.int32),
        ((PEERS * LANES,), jnp.int32),
    )
    codes, again = lax.optimization_barrier((codes, features))
    second = onward(again, -1)
    (own,) = beside(
        lambda: (exchange(pack(codes, (features,), 0, OWN, width)),), ((PEERS * OWN, rows, width), bf16)
    )
    own, first = lax.optimization_barrier((own, first))
    third = onward(first, 1)
    (near,) = beside(
        lambda: (exchange(pack(codes, (first, second), OWN, NEAR, width)),), ((PEERS * NEAR, rows, width), bf16)
    )
    near, third = lax.optimization_barrier((near, third))
    far = exchange(pack(codes, (third,), OWN + NEAR, FAR, width))
    aggregated = aggregate(pos, counts, own, near, far, tiles, node_cols)
    node_rows = lax.all_to_all(aggregated, ("zl", "y"), 0, 0).reshape(-1, node_cols)
    hidden, grad = dense(node_rows, w_neigh.T, self_part, cotangent)
    grad = fold(lax.all_to_all(grad, ("x", "c", "y"), 0, 0))
    grad = jnp.sum(lax.all_to_all(grad, "zl", 0, 0), axis=0)
    grad = jnp.transpose(grad.reshape(-1, ZH, rows), (1, 0, 2))
    grad = lax.all_to_all(jnp.pad(grad, ((0, 0), (0, 0), (0, LANES - rows))), "zh", 0, 0)
    grad_scale = 1.0 / math.sqrt(cols * X * ZH * CORE)
    return hidden, jnp.sum(grad, axis=0)[:, :rows] * grad_scale


def solution(mesh):
    fine = Mesh(mesh.devices.reshape(X, ZH, CORE, ZL, Y), ("x", "zh", "c", "zl", "y"))
    node, feat = ("x", "zh", "c"), ("zl", "y")
    return jax.shard_map(
        per_device,
        mesh=fine,
        in_specs=(
            P(feat, node),
            P(node),
            P(node, None),
            P(node),
            P(node, None, None),
            P(),
            P(None, node + feat),
            P(None, node + feat),
        ),
        out_specs=(P(None, node + feat), P(feat, node)),
        check_vma=False,
    )
```
